512 devices in a mesh: chan: 16 (over y, z_lo), tm: 32 (over x, z_hi, core).
Axes of the slice: x: 4, y: 8, z: 8 (z_hi: 4, z_lo: 2; z = z_hi * 2 + z_lo), core: 2. Of those that a mesh axis runs over, the one named last changes fastest.
Arguments:
- spectra: bfloat16 [32, 512, 2, 2048], P('tm', 'chan'), may hold values from -420 to 420
- window_valid: int32 [32], P('tm'), may hold values 0 or 1
- pair_code: int32 [16, 32], P('chan'), may hold values from 0 to 143, as said below
- block_owner: int32 [16, 32], P('chan'), may hold values from 0 to 31, as said below
Outputs:
- stacks: float32 [16, 64, 8, 2048], P('chan', 'tm')
The draws below stay inside these ranges and needn't reach their ends.
Inputs may be any that keep to these rules, and one draw needn't show every extreme that they name: `pair_code`: each code is r * 9 * 4 + d * 4 + s with r, s < 4 and d < 9; the 32 codes of a group are distinct. `block_owner`: no index keeps more than 2 blocks of one group.
All inputs are finite; a program needn't handle non-finite values. No bound on the sum of `window_valid` on one device may be relied on, other than what follows from the above.
Results may differ from the reference program's by a relative error of at most 0.0021.
Values may be sent and summed in bfloat16 or wider, within the bound.
No kernel may reach another device: no remote copies, remote signals or barrier semaphores. Data moves between devices by JAX's collectives and lax.ppermute only.
A program may use at most 64 MiB of HBM per device.

```python
import math
import jax
import jax.numpy as jnp
from jax import lax

F = 2048
CB = 8
G = 4
LAGS = 256
SLOTS = 2
CG = 32
GROUPS = 16
NCH = 512
NW = 32
DIST = 9
NBLK = 32
N_TM = 32


def draw_spectra(key, part):
    keys = jax.random.split(key, 3)
    shape = (NW, NCH, 2, F)
    row_scale = jnp.exp(jax.random.uniform(keys[1], (NW, NCH, 1, 1), jnp.float32) * math.log(10.0))
    bin_scale = jnp.exp(jax.random.uniform(keys[2], (1, NCH, 1, F), jnp.float32) * math.log(10.0))
    base = jnp.clip(jax.random.normal(keys[0], shape, jnp.float32), -4.0, 4.0)
    return (base * row_scale * bin_scale).astype(jnp.bfloat16)


def draw_pair_code(key, part):
    total = G * DIST * G

    def one_group(group_key):
        first_key, second_key = jax.random.split(group_key)
        middle = jax.random.permutation(first_key, total - 2) + 1
        picks = jnp.concatenate([jnp.array([0, total - 1], jnp.int32), middle[:NBLK - 2].astype(jnp.int32)])
        return jax.random.permutation(second_key, picks)
    group_keys = jax.random.split(jax.random.fold_in(key, 11), GROUPS)
    return jax.vmap(one_group)(group_keys).astype(jnp.int32)


def draw_owner_group(group_key):
    keys = jax.random.split(group_key, 3)
    slot_ids = jnp.arange(SLOTS * NBLK, dtype=jnp.int32)
    full_owner = jax.random.randint(keys[0], (), 1, NBLK - 1)
    forced = (slot_ids // SLOTS == full_owner) | (slot_ids == 0) | (slot_ids == (NBLK - 1) * SLOTS)
    scores = jax.random.permutation(keys[1], SLOTS * NBLK).astype(jnp.int32)
    scores = jnp.where(forced, scores - SLOTS * NBLK, scores)
    order = jnp.argsort(scores, stable=True)
    chosen = slot_ids[order[:NBLK]]
    return jax.random.permutation(keys[2], chosen // SLOTS)


def draw_block_owner(key, part):
    group_keys = jax.random.split(jax.random.fold_in(key, 23), GROUPS)
    return jax.vmap(draw_owner_group)(group_keys).astype(jnp.int32)


def with_ends(drawn, own_key, low, top_value):
    dims = drawn.shape
    spot = [jax.random.randint(jax.random.fold_in(own_key, axis), (), 0, dims[axis]) for axis in range(len(dims))]
    drawn = drawn.at[tuple(spot)].set(low)
    longest = dims.index(max(dims))
    spot[longest] = (spot[longest] + 1) % dims[longest]
    return drawn.at[tuple(spot)].set(top_value)


def setup_inputs(seed: int = 0) -> dict:
    streams_of = jax.random.split(jax.random.key(seed), 5)
    return {
        "spectra": draw_spectra(jax.random.fold_in(streams_of[4], 71), 0),
        "window_valid": with_ends((jax.random.randint(streams_of[1], (NW,), 0, 4) < 3).astype(jnp.int32), jax.random.fold_in(streams_of[1], 1), 0, 1),
        "pair_code": draw_pair_code(jax.random.fold_in(streams_of[4], 71), 0),
        "block_owner": draw_block_owner(jax.random.fold_in(streams_of[4], 71), 0),
    }


EPS = 1e-05

def lag_tables(freq_bins, lag_count):
    freq_index = jnp.arange(freq_bins, dtype=jnp.int32)[:, None]
    shifts = jnp.arange(lag_count, dtype=jnp.int32)[None, :] - lag_count // 2
    phase_int = freq_index * shifts % (2 * freq_bins)
    angles = phase_int.astype(jnp.float32) * (math.pi / freq_bins)
    return (jnp.cos(angles), -jnp.sin(angles))

def reference(spectra, window_valid, pair_code, block_owner):
    cos_table, sin_table = lag_tables(F, LAGS)

    def whiten_row(slab_row):
        raw_values = slab_row.astype(jnp.float32)
        mean_power = lax.optimization_barrier(jnp.mean(raw_values * raw_values, axis=(1, 2), keepdims=True))
        return (raw_values * lax.rsqrt(mean_power + EPS)).astype(jnp.bfloat16)
    white = lax.map(whiten_row, spectra)
    weight = window_valid.astype(jnp.float32)[:, None, None]
    lag_scale = 1.0 / math.sqrt(F * NW)
    high = lax.Precision.HIGHEST

    def one_group(group):
        block_codes = pair_code[group]
        owners = block_owner[group]

        def one_block(code):
            near_blk = code // (DIST * G)
            dist_blk = code // G % DIST
            far_blk = code % G
            near_start = (group * CG + near_blk * CB).astype(jnp.int32)
            far_start = ((group + dist_blk) % GROUPS * CG + far_blk * CB).astype(jnp.int32)
            near_side = lax.dynamic_slice_in_dim(white, near_start, CB, 1).astype(jnp.float32)
            far_side = lax.dynamic_slice_in_dim(white, far_start, CB, 1).astype(jnp.float32)
            near_re = near_side[:, :, 0] * weight
            near_im = near_side[:, :, 1] * weight
            far_re = far_side[:, :, 0]
            far_im = far_side[:, :, 1]
            real_part = jnp.einsum('wif,wjf->ijf', near_re, far_re, precision=high) + jnp.einsum('wif,wjf->ijf', near_im, far_im, precision=high)
            imag_part = jnp.einsum('wif,wjf->ijf', near_im, far_re, precision=high) - jnp.einsum('wif,wjf->ijf', near_re, far_im, precision=high)
            lagged = jnp.dot(real_part.reshape(CB * CB, F), cos_table, precision=high, preferred_element_type=jnp.float32)
            lagged = lagged + jnp.dot(imag_part.reshape(CB * CB, F), sin_table, precision=high, preferred_element_type=jnp.float32)
            return (lagged * lag_scale).reshape(CB, CB * LAGS)
        lagged_all = lax.map(one_block, block_codes)
        order_index = jnp.arange(NBLK, dtype=jnp.int32)
        earlier = order_index[None, :] < order_index[:, None]
        same_owner = owners[None, :] == owners[:, None]
        slot_rank = lax.optimization_barrier(jnp.sum((earlier & same_owner).astype(jnp.int32), axis=1))
        slot_index = (owners * SLOTS + slot_rank).astype(jnp.int32)
        empty = jnp.zeros((N_TM * SLOTS, CB, CB * LAGS), jnp.float32)
        return empty.at[slot_index].set(lagged_all)
    return lax.map(one_group, jnp.arange(GROUPS, dtype=jnp.int32))
```

```python
import functools
import math

import jax
import jax.numpy as jnp
import numpy as np
from jax import lax
from jax.experimental import pallas as pl
from jax.experimental.pallas import tpu as pltpu
from jax.sharding import PartitionSpec as P

CB = 8
G = 4
CG = G * CB
LAGS = 256
SLOTS = 2
EPS = 1e-05
GROUPS = 16
WIN = 32
F = 2048
JJ = 4
PHI = F // JJ
MESSAGE = JJ * 2 * CG

BF16 = jnp.bfloat16
F32 = jnp.float32


def params():
    return pltpu.CompilerParams(vmem_limit_bytes=40 << 20)


def whiten_kernel(x_ref, valid_ref, out_ref):
    raw = x_ref[...].astype(F32)
    squares = jnp.sum(raw * raw, axis=(0, 2), keepdims=True)
    mean_power = squares * (1.0 / (2 * F))
    white = (raw * lax.rsqrt(mean_power + EPS)).astype(BF16).astype(F32)
    white = white * valid_ref[0].astype(F32)
    white = white.reshape(2 * CG, F)
    for pair in range(JJ // 2):
        rows = jnp.concatenate(
            [white[:, (2 * pair + j) * PHI : (2 * pair + j + 1) * PHI] for j in range(2)], axis=0
        )
        out_ref[:, pair * 128 : (pair + 1) * 128] = rows.T.astype(BF16)


def whiten(spectra, valid):
    return pl.pallas_call(
        whiten_kernel,
        out_shape=jax.ShapeDtypeStruct((PHI, MESSAGE), BF16),
        in_specs=[
            pl.BlockSpec(memory_space=pltpu.VMEM),
            pl.BlockSpec(memory_space=pltpu.SMEM),
        ],
        out_specs=pl.BlockSpec(memory_space=pltpu.VMEM),
        compiler_params=params(),
    )(spectra, valid)


def near_tables():
    far_re = np.zeros((MESSAGE, 256), np.float32)
    far_im = np.zeros((MESSAGE, 256), np.float32)
    for r in range(G):
        for j in range(JJ):
            for i in range(CB):
                re_row = (j * 2) * CG + r * CB + i
                im_row = re_row + CG
                re_lane = r * 64 + (j * 2) * CB + i
                im_lane = re_lane + CB
                far_re[re_row, re_lane] = 1
                far_re[im_row, im_lane] = 1
                far_im[im_row, re_lane] = 1
                far_im[re_row, im_lane] = -1
    return far_re, far_im


def cross_kernel(r_ref, slots_ref, near_re_ref, near_im_ref, out_ref, far_ref, near_ref):
    quarter = lax.broadcasted_iota(jnp.int32, (32, 128), 1) // 32
    for g4 in range(GROUPS // 4):
        for q4 in range(2):
            block = r_ref[g4 * 128 : (g4 + 1) * 128, q4 * 128 : (q4 + 1) * 128].astype(F32)
            turned = block.T
            for g in range(4):
                rows = None
                for q in range(4):
                    piece = turned[q * 32 : (q + 1) * 32, :]
                    shift = ((q - g) * 32) % 128
                    if shift:
                        piece = pltpu.roll(piece, shift, 1)
                    rows = piece if rows is None else jnp.where(quarter == q, piece, rows)
                start = (g4 * 4 + g) * 32
                far_ref[start : start + 32, q4 * 128 : (q4 + 1) * 128] = rows.astype(BF16)
    lane_j = lax.broadcasted_iota(jnp.int32, (32, 256), 1) // 16 % JJ
    for part, table in enumerate((near_re_ref, near_im_ref)):
        spread = jnp.dot(r_ref[...], table[...], preferred_element_type=F32)
        for g in range(GROUPS):
            rows = spread[g * 32 : (g + 1) * 32]
            for j in range(JJ):
                start = (j * 2 + part) * 32
                near_ref[g, start : start + 32, :] = jnp.where(lane_j == j, rows, 0.0).astype(BF16)

    lanes = lax.broadcasted_iota(jnp.int32, (512, 512), 1)
    first_half = lax.broadcasted_iota(jnp.int32, (256, 128), 1) < 64

    def one_group(g, _):
        slots = pltpu.roll(slots_ref[...], jnp.where(g == 0, 0, 128 - g), 1)
        slot = slots[:, 0:1]
        far_row = slot >> 2
        near_blk = slot & 3
        pick = jnp.where(lanes == far_row, 1.0, 0.0).astype(BF16)
        far = jnp.dot(pick, far_ref[...], preferred_element_type=F32).astype(BF16)
        cross = jnp.dot(far, near_ref[g], preferred_element_type=F32)
        half = jnp.where(near_blk >= 2, cross[:, 128:], cross[:, :128])
        turned = pltpu.roll(half, 64, 1)
        odd = (near_blk & 1) == 1
        low = jnp.where(odd, turned, half)[:256]
        high = jnp.where(odd, half, turned)[256:]
        start = pl.multiple_of(g * 256, 256)
        out_ref[pl.ds(start, 256), :] = jnp.where(first_half, low, high).astype(BF16)
        return 0

    lax.fori_loop(0, GROUPS, one_group, 0)


def cross(received, slots):
    near_re, near_im = (jnp.asarray(t, BF16) for t in near_tables())
    return pl.pallas_call(
        cross_kernel,
        out_shape=jax.ShapeDtypeStruct((GROUPS * 32 * CB, 128), BF16),
        in_specs=[pl.BlockSpec(memory_space=pltpu.VMEM)] * 4,
        out_specs=pl.BlockSpec(memory_space=pltpu.VMEM),
        scratch_shapes=[
            pltpu.VMEM((512, 256), BF16),
            pltpu.VMEM((GROUPS, 256, 256), BF16),
        ],
        compiler_params=params(),
    )(received, slots, near_re, near_im)


def lag_tables():
    shifts = np.arange(LAGS) - LAGS // 2
    angle = np.pi / F * (np.arange(PHI)[:, None] * shifts[None, :] % (2 * F))
    base = np.concatenate([np.cos(angle), np.sin(angle)], axis=1)
    high = base.astype(jnp.bfloat16)
    low = (base - high.astype(np.float64)).astype(jnp.bfloat16)
    turn = np.pi / F * (PHI * np.arange(JJ)[:, None] * shifts[None, :] % (2 * F))
    cos, sin = np.cos(turn), np.sin(turn)
    mix = np.stack([np.stack([cos, -sin], 1), np.stack([-sin, -cos], 1)], 1)
    mix = mix.reshape(JJ * 2 * 2, LAGS) / math.sqrt(F * WIN)
    return high, low, mix.astype(np.float32)


def lag_kernel(m_ref, high_ref, low_ref, mix_ref, out_ref, wide_ref, turned_ref):
    wide_ref[...] = m_ref[...].astype(F32)
    for far in range(CB):
        rows = wide_ref[pl.ds(far, PHI, stride=CB), :]
        turned_ref[far * 128 : (far + 1) * 128, :] = rows.T.astype(BF16)
    sums = jnp.dot(turned_ref[...], high_ref[...], preferred_element_type=F32)
    sums = sums + jnp.dot(turned_ref[...], low_ref[...], preferred_element_type=F32)
    for far in range(CB):
        for slot in range(SLOTS):
            total = None
            for q in range(JJ * 2):
                start = far * 128 + slot * 64 + q * CB
                rows = sums[start : start + CB]
                term = rows[:, :LAGS] * mix_ref[2 * q : 2 * q + 1, :]
                term = term + rows[:, LAGS:] * mix_ref[2 * q + 1 : 2 * q + 2, :]
                total = term if total is None else total + term
            out_ref[slot, :, far * LAGS : (far + 1) * LAGS] = total


def lags(arrived):
    high, low, mix = lag_tables()
    return pl.pallas_call(
        lag_kernel,
        out_shape=jax.ShapeDtypeStruct((SLOTS, CB, CB * LAGS), F32),
        in_specs=[pl.BlockSpec(memory_space=pltpu.VMEM)] * 4,
        out_specs=pl.BlockSpec(memory_space=pltpu.VMEM),
        scratch_shapes=[
            pltpu.VMEM((PHI * CB, 128), F32),
            pltpu.VMEM((CB * 128, PHI), BF16),
        ],
        compiler_params=params(),
    )(arrived, jnp.asarray(high), jnp.asarray(low), jnp.asarray(mix))


def slot_rows(pair_code, block_owner):
    codes = pair_code[0]
    owners = block_owner[0]
    blocks = codes.shape[0]
    order = jnp.arange(blocks, dtype=jnp.int32)
    earlier = order[None, :] < order[:, None]
    rank = jnp.sum((earlier & (owners[None, :] == owners[:, None])).astype(jnp.int32), axis=1)
    spot = rank * 32 + owners
    filled = spot[None, :] == jnp.arange(SLOTS * 32, dtype=jnp.int32)[:, None]
    mine = jnp.max(jnp.where(filled, codes[None, :] + 1, 0), axis=1)
    group = lax.axis_index("chan")
    groups = jnp.arange(GROUPS, dtype=jnp.int32)
    placed = jnp.where(groups[:, None] == group, mine[None, :], 0).astype(F32)
    table = lax.psum(placed, "chan").astype(jnp.int32).T
    code = table - 1
    near_blk = code // 36
    dist = code // 4 % 9
    far_blk = code % 4
    far_row = (groups[None, :] + dist) % GROUPS * CG + far_blk * CB
    base = far_row * 4 + near_blk
    inner = jnp.arange(CB, dtype=jnp.int32)[None, :, None] * 4
    rows = jnp.where(table[:, None, :] > 0, base[:, None, :] + inner, -1)
    rows = rows.reshape(SLOTS * 32 * CB, GROUPS)
    return jnp.pad(rows, ((0, 0), (0, 128 - GROUPS)))


def local(spectra, window_valid, pair_code, block_owner):
    both = ("chan", "tm")
    slots = slot_rows(pair_code, block_owner)
    parts_first = spectra[0].transpose(1, 0, 2)
    sent = whiten(parts_first, window_valid).reshape(PHI, 2, 128)
    received = lax.all_to_all(sent, both, 0, 0, tiled=True).reshape(GROUPS * WIN, MESSAGE)
    crossed = cross(received, slots).reshape(GROUPS * 32, CB, 128)
    arrived = lax.all_to_all(crossed, both, 0, 0, tiled=True).reshape(PHI * CB, 128)
    return lags(arrived)[None]


def solution(mesh):
    return jax.shard_map(
        local,
        mesh=mesh,
        in_specs=(P("tm", "chan", None, None), P("tm"), P("chan", None), P("chan", None)),
        out_specs=P("chan", "tm", None, None),
        check_vma=False,
    )
```

```python
import math

import jax
import jax.numpy as jnp
import numpy as np
from jax import lax
from jax.experimental import pallas as pl
from jax.experimental.pallas import tpu as pltpu
from jax.sharding import PartitionSpec as P

CB = 8
G = 4
CG = G * CB
LAGS = 256
SLOTS = 2
EPS = 1e-05
GROUPS = 16
WIN = 32
BLOCKS = 32
F = 2048
JJ = 4
PHI = F // JJ
MESSAGE = JJ * 2 * CG
ROWS = 4

BF16 = jnp.bfloat16
F32 = jnp.float32


def params():
    return pltpu.CompilerParams(vmem_limit_bytes=40 << 20)


def whiten_kernel(x_ref, valid_ref, code_ref, owner_ref, out_ref, wide_ref, sent_ref):
    wide_ref[...] = x_ref[...].astype(F32)
    tiles = F // 128
    raw = [
        [wide_ref[pl.ds(tile * 2 + part, CG, stride=tiles * 2), :] for tile in range(tiles)]
        for part in range(2)
    ]
    squares = sum(block * block for side in raw for block in side)
    mean_power = jnp.sum(squares, axis=1, keepdims=True) * (1.0 / (2 * F))
    scale = lax.rsqrt(mean_power + EPS)
    valid = valid_ref[0].astype(F32)
    for pair in range(JJ // 2):
        for tile in range(PHI // 128):
            rows = jnp.concatenate(
                [
                    (raw[part][j * (PHI // 128) + tile] * scale).astype(BF16).astype(F32) * valid
                    for j in (2 * pair, 2 * pair + 1)
                    for part in range(2)
                ],
                axis=0,
            )
            sent_ref[pl.ds(tile * 128 * ROWS + pair, 128, stride=ROWS), :] = rows.T
    code = code_ref[...]
    owner = owner_ref[...]
    near_blk = code // 36
    lane = lax.broadcasted_iota(jnp.int32, (1, 128), 1)
    lone = jnp.concatenate([owner, jnp.full((1, 128 - BLOCKS), -1, jnp.int32)], axis=1)
    rank = jnp.zeros((1, 128), jnp.int32)
    for back in range(1, BLOCKS):
        same = pltpu.roll(lone, back, 1) == lone
        rank = rank + jnp.where(same & (lane >= back), 1, 0)
    fields = jnp.concatenate([code - near_blk * 36, near_blk, owner, rank[:, :BLOCKS]], axis=1)
    fields = jnp.broadcast_to(fields.astype(F32), (PHI, 128))
    sent_ref[pl.ds(2, PHI, stride=ROWS), :] = fields
    sent_ref[pl.ds(3, PHI, stride=ROWS), :] = fields
    out_ref[...] = sent_ref[...].astype(BF16)


def whiten(spectra, valid, codes, owners):
    vmem = pl.BlockSpec(memory_space=pltpu.VMEM)
    return pl.pallas_call(
        whiten_kernel,
        out_shape=jax.ShapeDtypeStruct((PHI * ROWS, 128), BF16),
        in_specs=[vmem, pl.BlockSpec(memory_space=pltpu.SMEM), vmem, vmem],
        out_specs=vmem,
        scratch_shapes=[
            pltpu.VMEM((CG * F // 64, 128), F32),
            pltpu.VMEM((PHI * ROWS, 128), F32),
        ],
        compiler_params=params(),
    )(spectra, valid, codes, owners)


def near_tables():
    far_re = np.zeros((MESSAGE, 256), np.float32)
    far_im = np.zeros((MESSAGE, 256), np.float32)
    for r in range(G):
        for j in range(JJ):
            for i in range(CB):
                re_row = (j * 2) * CG + r * CB + i
                im_row = re_row + CG
                re_lane = r * 64 + (j * 2) * CB + i
                im_lane = re_lane + CB
                far_re[re_row, re_lane] = 1
                far_re[im_row, im_lane] = 1
                far_im[im_row, re_lane] = 1
                far_im[re_row, im_lane] = -1
    return far_re, far_im


def cross_kernel(
    r_ref,
    blocks_ref,
    near_re_ref,
    near_im_ref,
    out_ref,
    wide_ref,
    own_ref,
    far_ref,
    near_ref,
    slots_ref,
):
    slots_ref[...] = jnp.zeros_like(slots_ref)
    wide_ref[...] = r_ref[...].astype(F32)
    quarter = lax.broadcasted_iota(jnp.int32, (32, 128), 1) // 32
    for g4 in range(GROUPS // 4):
        for q4 in range(2):
            block = wide_ref[pl.ds(g4 * 128 * ROWS + q4, 128, stride=ROWS), :]
            own_ref[g4 * 128 : (g4 + 1) * 128, q4 * 128 : (q4 + 1) * 128] = block.astype(BF16)
            turned = block.T
            for g in range(4):
                rows = None
                for q in range(4):
                    piece = turned[q * 32 : (q + 1) * 32, :]
                    shift = ((q - g) * 32) % 128
                    if shift:
                        piece = pltpu.roll(piece, shift, 1)
                    rows = piece if rows is None else jnp.where(quarter == q, piece, rows)
                start = (g4 * 4 + g) * 32
                far_ref[start : start + 32, q4 * 128 : (q4 + 1) * 128] = rows
    lane_j = lax.broadcasted_iota(jnp.int32, (32, 256), 1) // 16 % JJ
    for part, table in enumerate((near_re_ref, near_im_ref)):
        spread = jnp.dot(own_ref[...], table[...], preferred_element_type=F32)
        for g in range(GROUPS):
            rows = spread[g * 32 : (g + 1) * 32]
            for j in range(JJ):
                start = (j * 2 + part) * 32
                near_ref[g, start : start + 32, :] = jnp.where(lane_j == j, rows, 0.0).astype(BF16)

    def one_group(g, _):
        entries = [blocks_ref[g, k] for k in range(BLOCKS)]
        far = jnp.concatenate(
            [
                far_ref[pl.ds(pl.multiple_of(((g * G + (e >> 8)) & 63) * CB, CB), CB), :]
                for e in entries
            ],
            axis=0,
        ).astype(BF16)
        cross = jnp.dot(far, near_ref[g], preferred_element_type=F32)
        for k, e in enumerate(entries):
            near_blk, owner, slot = (e >> 6) & 3, (e >> 1) & 31, e & 1
            rows = cross[k * CB : (k + 1) * CB]
            half = jnp.where(near_blk >= 2, rows[:, 128:], rows[:, :128])
            half = jnp.where((near_blk & 1) != slot, pltpu.roll(half, 64, 1), half)
            start = pl.multiple_of((g * 32 + owner) * CB, CB)
            slots_ref[slot, pl.ds(start, CB), :] = half
        return 0

    lax.fori_loop(0, GROUPS, one_group, 0)
    first_half = lax.broadcasted_iota(jnp.int32, (256, 128), 1) < 64

    def finish(g, _):
        rows = pl.ds(pl.multiple_of(g * 256, 256), 256)
        both = jnp.where(first_half, slots_ref[0, rows, :], slots_ref[1, rows, :])
        out_ref[rows, :] = both.astype(BF16)
        return 0

    lax.fori_loop(0, GROUPS, finish, 0)


def cross(received, blocks):
    near_re, near_im = (jnp.asarray(t, BF16) for t in near_tables())
    vmem = pl.BlockSpec(memory_space=pltpu.VMEM)
    return pl.pallas_call(
        cross_kernel,
        out_shape=jax.ShapeDtypeStruct((GROUPS * 32 * CB, 128), BF16),
        in_specs=[vmem, pl.BlockSpec(memory_space=pltpu.SMEM), vmem, vmem],
        out_specs=vmem,
        scratch_shapes=[
            pltpu.VMEM((GROUPS * WIN * ROWS, 128), F32),
            pltpu.VMEM((512, 256), BF16),
            pltpu.VMEM((512, 256), F32),
            pltpu.VMEM((GROUPS, 256, 256), BF16),
            pltpu.VMEM((SLOTS, GROUPS * 32 * CB, 128), F32),
        ],
        compiler_params=params(),
    )(received, blocks, near_re, near_im)


def lag_tables():
    shifts = np.arange(LAGS) - LAGS // 2
    angle = np.pi / F * (np.arange(PHI)[:, None] * shifts[None, :] % (2 * F))
    base = np.concatenate([np.cos(angle), np.sin(angle)], axis=1)
    high = base.astype(jnp.bfloat16)
    low = (base - high.astype(np.float64)).astype(jnp.bfloat16)
    turn = np.pi / F * (PHI * np.arange(JJ)[:, None] * shifts[None, :] % (2 * F))
    cos, sin = np.cos(turn), np.sin(turn)
    mix = np.stack([np.stack([cos, -sin], 1), np.stack([-sin, -cos], 1)], 1)
    mix = mix.reshape(JJ * 2 * 2, LAGS) / math.sqrt(F * WIN)
    return high, low, mix.astype(np.float32)


def lag_kernel(m_ref, high_ref, low_ref, mix_ref, out_ref, wide_ref, turned_ref):
    wide_ref[...] = m_ref[...].astype(F32)
    for far in range(CB):
        rows = wide_ref[pl.ds(far, PHI, stride=CB), :]
        turned_ref[far * 128 : (far + 1) * 128, :] = rows.T.astype(BF16)
    sums = jnp.dot(turned_ref[...], high_ref[...], preferred_element_type=F32)
    sums = sums + jnp.dot(turned_ref[...], low_ref[...], preferred_element_type=F32)
    for far in range(CB):
        for slot in range(SLOTS):
            total = None
            for q in range(JJ * 2):
                start = far * 128 + slot * 64 + q * CB
                rows = sums[start : start + CB]
                term = rows[:, :LAGS] * mix_ref[2 * q : 2 * q + 1, :]
                term = term + rows[:, LAGS:] * mix_ref[2 * q + 1 : 2 * q + 2, :]
                total = term if total is None else total + term
            out_ref[slot, :, far * LAGS : (far + 1) * LAGS] = total


def lags(arrived):
    high, low, mix = lag_tables()
    return pl.pallas_call(
        lag_kernel,
        out_shape=jax.ShapeDtypeStruct((SLOTS, CB, CB * LAGS), F32),
        in_specs=[pl.BlockSpec(memory_space=pltpu.VMEM)] * 4,
        out_specs=pl.BlockSpec(memory_space=pltpu.VMEM),
        scratch_shapes=[
            pltpu.VMEM((PHI * CB, 128), F32),
            pltpu.VMEM((CB * 128, PHI), BF16),
        ],
        compiler_params=params(),
    )(arrived, jnp.asarray(high), jnp.asarray(low), jnp.asarray(mix))


def local(spectra, window_valid, pair_code, block_owner):
    both = ("chan", "tm")
    tiled = spectra.reshape(CG, 2, F // 128, 128).transpose(0, 2, 1, 3).reshape(CG * F // 64, 128)
    sent = whiten(tiled, window_valid, pair_code, block_owner).reshape(PHI, ROWS, 128)
    received = lax.all_to_all(sent, both, 0, 0, tiled=True)
    fields = received[::WIN, 2].astype(jnp.int32)
    far, near, owner, rank = (fields[:, i * BLOCKS : (i + 1) * BLOCKS] for i in range(4))
    blocks = far * 256 + near * 64 + owner * 2 + rank
    crossed = cross(received.reshape(GROUPS * WIN * ROWS, 128), blocks)
    crossed = crossed.reshape(GROUPS * 32, CB, 128)
    arrived = lax.all_to_all(crossed, both, 0, 0, tiled=True).reshape(PHI * CB, 128)
    return lags(arrived)[None]


def solution(mesh):
    return jax.shard_map(
        local,
        mesh=mesh,
        in_specs=(P("tm", "chan", None, None), P("tm"), P("chan", None), P("chan", None)),
        out_specs=P("chan", "tm", None, None),
        check_vma=False,
    )
```

```python
import math

import jax
import jax.numpy as jnp
import numpy as np
from jax import lax
from jax.experimental import pallas as pl
from jax.experimental.pallas import tpu as pltpu
from jax.sharding import PartitionSpec as P

CB = 8
G = 4
CG = G * CB
LAGS = 256
SLOTS = 2
EPS = 1e-05
GROUPS = 16
WIN = 32
BLOCKS = 32
F = 2048
JJ = 4
PHI = F // JJ
MESSAGE = JJ * 2 * CG
ROWS = 4

BF16 = jnp.bfloat16
F32 = jnp.float32


def params():
    return pltpu.CompilerParams(vmem_limit_bytes=40 << 20)


def sent_fields(code_ref, owner_ref, sent_ref):
    lane = lax.broadcasted_iota(jnp.int32, (1, 128), 1)
    fill = jnp.full((1, 128 - BLOCKS), -1, jnp.int32)
    owner = jnp.concatenate([owner_ref[...], fill], axis=1)
    code = jnp.concatenate([code_ref[...], fill], axis=1)
    rank = jnp.zeros((1, 128), jnp.int32)
    for back in range(1, BLOCKS):
        same = pltpu.roll(owner, back, 1) == owner
        rank = rank + jnp.where(same & (lane >= back), 1, 0)
    near_blk = code // 36
    far = code - near_blk * 36
    form = ((near_blk >> 1) + 2 * ((near_blk & 1) ^ rank)) * BLOCKS + lane
    place = rank * 32 + owner
    fields = jnp.where(lane < BLOCKS, far, pltpu.roll(form, BLOCKS, 1))
    fields = jnp.where(lane < 2 * BLOCKS, fields, pltpu.roll(place, 2 * BLOCKS, 1))
    fields = jnp.where(lane < 3 * BLOCKS, fields, 0)
    fields = jnp.broadcast_to(fields.astype(F32), (PHI, 128))
    sent_ref[pl.ds(2, PHI, stride=ROWS), :] = fields
    sent_ref[pl.ds(3, PHI, stride=ROWS), :] = fields


def whiten_kernel(x_ref, valid_ref, code_ref, owner_ref, out_ref, wide_ref, sent_ref):
    sent_fields(code_ref, owner_ref, sent_ref)
    wide_ref[...] = x_ref[...].astype(F32)
    tiles = F // 128
    raw = [
        [wide_ref[pl.ds(tile * 2 + part, CG, stride=tiles * 2), :] for tile in range(tiles)]
        for part in range(2)
    ]
    squares = sum(block * block for side in raw for block in side)
    mean_power = jnp.sum(squares, axis=1, keepdims=True) * (1.0 / (2 * F))
    scale = lax.rsqrt(mean_power + EPS)
    valid = valid_ref[0].astype(F32)
    for pair in range(JJ // 2):
        for tile in range(PHI // 128):
            rows = jnp.concatenate(
                [
                    (raw[part][j * (PHI // 128) + tile] * scale).astype(BF16).astype(F32) * valid
                    for j in (2 * pair, 2 * pair + 1)
                    for part in range(2)
                ],
                axis=0,
            )
            sent_ref[pl.ds(tile * 128 * ROWS + pair, 128, stride=ROWS), :] = rows.T
    out_ref[...] = sent_ref[...].astype(BF16)


def whiten(spectra, valid, codes, owners):
    vmem = pl.BlockSpec(memory_space=pltpu.VMEM)
    return pl.pallas_call(
        whiten_kernel,
        out_shape=jax.ShapeDtypeStruct((PHI * ROWS, 128), BF16),
        in_specs=[vmem, pl.BlockSpec(memory_space=pltpu.SMEM), vmem, vmem],
        out_specs=vmem,
        scratch_shapes=[
            pltpu.VMEM((CG * F // 64, 128), F32),
            pltpu.VMEM((PHI * ROWS, 128), F32),
        ],
        compiler_params=params(),
    )(spectra, valid, codes, owners)


def near_tables():
    far_re = np.zeros((MESSAGE, 256), np.float32)
    far_im = np.zeros((MESSAGE, 256), np.float32)
    for r in range(G):
        for j in range(JJ):
            for i in range(CB):
                re_row = (j * 2) * CG + r * CB + i
                im_row = re_row + CG
                re_lane = r * 64 + (j * 2) * CB + i
                im_lane = re_lane + CB
                far_re[re_row, re_lane] = 1
                far_re[im_row, im_lane] = 1
                far_im[im_row, re_lane] = 1
                far_im[re_row, im_lane] = -1
    return far_re, far_im


def cross_kernel(
    r_ref, blocks_ref, near_re_ref, near_im_ref, out_ref, wide_ref, own_ref, far_ref, near_ref, forms_ref, slots_ref
):
    slots_ref[...] = jnp.zeros_like(slots_ref)
    wide_ref[...] = r_ref[...].astype(F32)
    quarter = lax.broadcasted_iota(jnp.int32, (32, 128), 1) // 32
    for g4 in range(GROUPS // 4):
        for q4 in range(2):
            block = wide_ref[pl.ds(g4 * 128 * ROWS + q4, 128, stride=ROWS), :]
            own_ref[g4 * 128 : (g4 + 1) * 128, q4 * 128 : (q4 + 1) * 128] = block.astype(BF16)
            turned = block.T
            for g in range(4):
                rows = None
                for q in range(4):
                    piece = turned[q * 32 : (q + 1) * 32, :]
                    shift = ((q - g) * 32) % 128
                    if shift:
                        piece = pltpu.roll(piece, shift, 1)
                    rows = piece if rows is None else jnp.where(quarter == q, piece, rows)
                start = (g4 * 4 + g) * 32
                far_ref[start : start + 32, q4 * 128 : (q4 + 1) * 128] = rows
    for part, table in enumerate((near_re_ref, near_im_ref)):
        spread = jnp.dot(own_ref[...], table[...], preferred_element_type=F32)
        near_ref[part] = spread.astype(BF16)

    lane_j = lax.broadcasted_iota(jnp.int32, (32, 256), 1) // 16 % JJ
    keeps = [jnp.where(lane_j == j, 1.0, 0.0).astype(BF16) for j in range(JJ)]

    for g in range(GROUPS):
        far_rows = [(blocks_ref[g, k] + g * CG) & (GROUPS * CG - 1) for k in range(BLOCKS)]
        far = jnp.concatenate(
            [far_ref[pl.ds(pl.multiple_of(row, CB), CB), :] for row in far_rows], axis=0
        ).astype(BF16)
        sides = [near_ref[side, g * WIN : (g + 1) * WIN, :] for side in range(2)]
        near = jnp.concatenate([side * keep for keep in keeps for side in sides], axis=0)
        cross = jnp.dot(far, near, preferred_element_type=F32)
        for half in range(2):
            rows = cross[:, half * 128 : (half + 1) * 128]
            forms_ref[g, half * 256 : (half + 1) * 256, :] = rows
            forms_ref[g, (half + 2) * 256 : (half + 3) * 256, :] = pltpu.roll(rows, 64, 1)
        for k in range(BLOCKS):
            form = pl.multiple_of(blocks_ref[g, BLOCKS + k], CB)
            place = pl.multiple_of(blocks_ref[g, 2 * BLOCKS + k], CB)
            slots_ref[g, pl.ds(place, CB), :] = forms_ref[g, pl.ds(form, CB), :]
    first_half = lax.broadcasted_iota(jnp.int32, (256, 128), 1) < 64
    for g in range(GROUPS):
        low = slots_ref[g, :256, :]
        high = slots_ref[g, 256:, :]
        out_ref[g * 256 : (g + 1) * 256, :] = jnp.where(first_half, low, high).astype(BF16)


def cross(received, blocks):
    near_re, near_im = (jnp.asarray(t, BF16) for t in near_tables())
    vmem = pl.BlockSpec(memory_space=pltpu.VMEM)
    return pl.pallas_call(
        cross_kernel,
        out_shape=jax.ShapeDtypeStruct((GROUPS * 32 * CB, 128), BF16),
        in_specs=[vmem, pl.BlockSpec(memory_space=pltpu.SMEM), vmem, vmem],
        out_specs=vmem,
        scratch_shapes=[
            pltpu.VMEM((GROUPS * WIN * ROWS, 128), F32),
            pltpu.VMEM((512, 256), BF16),
            pltpu.VMEM((512, 256), F32),
            pltpu.VMEM((2, 512, 256), BF16),
            pltpu.VMEM((GROUPS, 4 * 256, 128), F32),
            pltpu.VMEM((GROUPS, SLOTS * 32 * CB, 128), F32),
        ],
        compiler_params=params(),
    )(received, blocks, near_re, near_im)


def lag_tables():
    shifts = np.arange(LAGS) - LAGS // 2
    angle = np.pi / F * (np.arange(PHI)[:, None] * shifts[None, :] % (2 * F))
    base = np.concatenate([np.cos(angle), np.sin(angle)], axis=1)
    high = base.astype(jnp.bfloat16)
    low = (base - high.astype(np.float64)).astype(jnp.bfloat16)
    turn = np.pi / F * (PHI * np.arange(JJ)[:, None] * shifts[None, :] % (2 * F))
    cos, sin = np.cos(turn), np.sin(turn)
    mix = np.stack([np.stack([cos, -sin], 1), np.stack([-sin, -cos], 1)], 1)
    mix = mix.reshape(JJ * 2 * 2, LAGS) / math.sqrt(F * WIN)
    return high, low, mix.astype(np.float32)


def lag_kernel(m_ref, high_ref, low_ref, mix_ref, out_ref, wide_ref, turned_ref):
    wide_ref[...] = m_ref[...].astype(F32)
    for far in range(CB):
        rows = wide_ref[pl.ds(far, PHI, stride=CB), :]
        turned_ref[far * 128 : (far + 1) * 128, :] = rows.T.astype(BF16)
    sums = jnp.dot(turned_ref[...], high_ref[...], preferred_element_type=F32)
    sums = sums + jnp.dot(turned_ref[...], low_ref[...], preferred_element_type=F32)
    for far in range(CB):
        for slot in range(SLOTS):
            total = None
            for q in range(JJ * 2):
                start = far * 128 + slot * 64 + q * CB
                rows = sums[start : start + CB]
                term = rows[:, :LAGS] * mix_ref[2 * q : 2 * q + 1, :]
                term = term + rows[:, LAGS:] * mix_ref[2 * q + 1 : 2 * q + 2, :]
                total = term if total is None else total + term
            out_ref[slot, :, far * LAGS : (far + 1) * LAGS] = total


def lags(arrived):
    high, low, mix = lag_tables()
    return pl.pallas_call(
        lag_kernel,
        out_shape=jax.ShapeDtypeStruct((SLOTS, CB, CB * LAGS), F32),
        in_specs=[pl.BlockSpec(memory_space=pltpu.VMEM)] * 4,
        out_specs=pl.BlockSpec(memory_space=pltpu.VMEM),
        scratch_shapes=[
            pltpu.VMEM((PHI * CB, 128), F32),
            pltpu.VMEM((CB * 128, PHI), BF16),
        ],
        compiler_params=params(),
    )(arrived, jnp.asarray(high), jnp.asarray(low), jnp.asarray(mix))


def local(spectra, window_valid, pair_code, block_owner):
    both = ("chan", "tm")
    tiled = spectra.reshape(CG, 2, F // 128, 128).transpose(0, 2, 1, 3).reshape(CG * F // 64, 128)
    sent = whiten(tiled, window_valid, pair_code, block_owner).reshape(PHI, ROWS, 128)
    received = lax.all_to_all(sent, both, 0, 0, tiled=True)
    blocks = received[::WIN, 2].astype(jnp.int32) * CB
    crossed = cross(received.reshape(GROUPS * WIN * ROWS, 128), blocks)
    crossed = crossed.reshape(GROUPS * 32, CB, 128)
    arrived = lax.all_to_all(crossed, both, 0, 0, tiled=True).reshape(PHI * CB, 128)
    return lags(arrived)[None]


def solution(mesh):
    return jax.shard_map(
        local,
        mesh=mesh,
        in_specs=(P("tm", "chan", None, None), P("tm"), P("chan", None), P("chan", None)),
        out_specs=P("chan", "tm", None, None),
        check_vma=False,
    )
```

```python
import math

import jax
import jax.numpy as jnp
import numpy as np
from jax import lax
from jax.experimental import pallas as pl
from jax.experimental.pallas import tpu as pltpu
from jax.sharding import PartitionSpec as P

CB = 8
G = 4
CG = G * CB
LAGS = 256
SLOTS = 2
EPS = 1e-05
GROUPS = 16
WIN = 32
BLOCKS = 32
F = 2048
JJ = 4
PHI = F // JJ
MESSAGE = JJ * 2 * CG
ROWS = 4

BF16 = jnp.bfloat16
F32 = jnp.float32


def params():
    return pltpu.CompilerParams(vmem_limit_bytes=40 << 20)


def sent_fields(code_ref, owner_ref, sent_ref):
    lane = lax.broadcasted_iota(jnp.int32, (1, 128), 1)
    fill = jnp.full((1, 128 - BLOCKS), -1, jnp.int32)
    owner = jnp.concatenate([owner_ref[...], fill], axis=1)
    code = jnp.concatenate([code_ref[...], fill], axis=1)
    rank = jnp.zeros((1, 128), jnp.int32)
    for back in range(1, BLOCKS):
        same = pltpu.roll(owner, back, 1) == owner
        rank = rank + jnp.where(same & (lane >= back), 1, 0)
    near_blk = code // 36
    far = code - near_blk * 36
    form = ((near_blk >> 1) + 2 * ((near_blk & 1) ^ rank)) * BLOCKS + lane
    place = rank * 32 + owner
    fields = jnp.where(lane < BLOCKS, far, pltpu.roll(form, BLOCKS, 1))
    fields = jnp.where(lane < 2 * BLOCKS, fields, pltpu.roll(place, 2 * BLOCKS, 1))
    fields = jnp.where(lane < 3 * BLOCKS, fields, 0)
    fields = jnp.broadcast_to(fields.astype(F32), (PHI, 128))
    sent_ref[pl.ds(2, PHI, stride=ROWS), :] = fields
    sent_ref[pl.ds(3, PHI, stride=ROWS), :] = fields


def whiten_kernel(
    x_hbm, valid_ref, code_hbm, owner_hbm, out_ref, x_ref, code_ref, owner_ref, wide_ref, sent_ref, sems
):
    copies = [
        pltpu.make_async_copy(source, target, sems.at[i])
        for i, (source, target) in enumerate(
            ((x_hbm, x_ref), (code_hbm, code_ref), (owner_hbm, owner_ref))
        )
    ]
    for copy in copies:
        copy.start()
    for copy in copies[1:]:
        copy.wait()
    sent_fields(code_ref, owner_ref, sent_ref)
    copies[0].wait()
    wide_ref[...] = x_ref[...].astype(F32)
    tiles = F // 128
    raw = [
        [wide_ref[pl.ds(tile * 2 + part, CG, stride=tiles * 2), :] for tile in range(tiles)]
        for part in range(2)
    ]
    squares = sum(block * block for side in raw for block in side)
    mean_power = jnp.sum(squares, axis=1, keepdims=True) * (1.0 / (2 * F))
    scale = lax.rsqrt(mean_power + EPS)
    valid = valid_ref[0].astype(F32)
    for pair in range(JJ // 2):
        for tile in range(PHI // 128):
            rows = jnp.concatenate(
                [
                    (raw[part][j * (PHI // 128) + tile] * scale).astype(BF16).astype(F32) * valid
                    for j in (2 * pair, 2 * pair + 1)
                    for part in range(2)
                ],
                axis=0,
            )
            sent_ref[pl.ds(tile * 128 * ROWS + pair, 128, stride=ROWS), :] = rows.T
    out_ref[...] = sent_ref[...].astype(BF16)


def whiten(spectra, valid, codes, owners):
    there = pl.BlockSpec(memory_space=pl.ANY)
    return pl.pallas_call(
        whiten_kernel,
        out_shape=jax.ShapeDtypeStruct((PHI * ROWS, 128), BF16),
        in_specs=[there, pl.BlockSpec(memory_space=pltpu.SMEM), there, there],
        out_specs=pl.BlockSpec(memory_space=pltpu.VMEM),
        scratch_shapes=[
            pltpu.VMEM((CG * F // 64, 128), BF16),
            pltpu.VMEM((1, BLOCKS), jnp.int32),
            pltpu.VMEM((1, BLOCKS), jnp.int32),
            pltpu.VMEM((CG * F // 64, 128), F32),
            pltpu.VMEM((PHI * ROWS, 128), F32),
            pltpu.SemaphoreType.DMA((3,)),
        ],
        compiler_params=pltpu.CompilerParams(vmem_limit_bytes=62 << 20),
    )(spectra, valid, codes, owners)


def near_tables():
    far_re = np.zeros((MESSAGE, 256), np.float32)
    far_im = np.zeros((MESSAGE, 256), np.float32)
    for r in range(G):
        for j in range(JJ):
            for i in range(CB):
                re_row = (j * 2) * CG + r * CB + i
                im_row = re_row + CG
                re_lane = r * 64 + (j * 2) * CB + i
                im_lane = re_lane + CB
                far_re[re_row, re_lane] = 1
                far_re[im_row, im_lane] = 1
                far_im[im_row, re_lane] = 1
                far_im[re_row, im_lane] = -1
    return far_re, far_im


def cross_kernel(
    r_ref, blocks_ref, near_re_ref, near_im_ref, out_ref, wide_ref, own_ref, far_ref, near_ref, forms_ref, slots_ref
):
    slots_ref[...] = jnp.zeros_like(slots_ref)
    wide_ref[...] = r_ref[...].astype(F32)
    quarter = lax.broadcasted_iota(jnp.int32, (32, 128), 1) // 32
    for g4 in range(GROUPS // 4):
        for q4 in range(2):
            block = wide_ref[pl.ds(g4 * 128 * ROWS + q4, 128, stride=ROWS), :]
            own_ref[g4 * 128 : (g4 + 1) * 128, q4 * 128 : (q4 + 1) * 128] = block.astype(BF16)
            turned = block.T
            for g in range(4):
                rows = None
                for q in range(4):
                    piece = turned[q * 32 : (q + 1) * 32, :]
                    shift = ((q - g) * 32) % 128
                    if shift:
                        piece = pltpu.roll(piece, shift, 1)
                    rows = piece if rows is None else jnp.where(quarter == q, piece, rows)
                start = (g4 * 4 + g) * 32
                far_ref[start : start + 32, q4 * 128 : (q4 + 1) * 128] = rows
    for part, table in enumerate((near_re_ref, near_im_ref)):
        spread = jnp.dot(own_ref[...], table[...], preferred_element_type=F32)
        near_ref[part] = spread.astype(BF16)

    lane_j = lax.broadcasted_iota(jnp.int32, (32, 256), 1) // 16 % JJ
    keeps = [jnp.where(lane_j == j, 1.0, 0.0).astype(BF16) for j in range(JJ)]

    for g in range(GROUPS):
        far_rows = [(blocks_ref[g, k] + g * CG) & (GROUPS * CG - 1) for k in range(BLOCKS)]
        far = jnp.concatenate(
            [far_ref[pl.ds(pl.multiple_of(row, CB), CB), :] for row in far_rows], axis=0
        ).astype(BF16)
        sides = [near_ref[side, g * WIN : (g + 1) * WIN, :] for side in range(2)]
        near = jnp.concatenate([side * keep for keep in keeps for side in sides], axis=0)
        cross = jnp.dot(far, near, preferred_element_type=F32)
        for half in range(2):
            rows = cross[:, half * 128 : (half + 1) * 128]
            forms_ref[g, half * 256 : (half + 1) * 256, :] = rows
            forms_ref[g, (half + 2) * 256 : (half + 3) * 256, :] = pltpu.roll(rows, 64, 1)
        for k in range(BLOCKS):
            form = pl.multiple_of(blocks_ref[g, BLOCKS + k], CB)
            place = pl.multiple_of(blocks_ref[g, 2 * BLOCKS + k], CB)
            slots_ref[g, pl.ds(place, CB), :] = forms_ref[g, pl.ds(form, CB), :]
    first_half = lax.broadcasted_iota(jnp.int32, (256, 128), 1) < 64
    for g in range(GROUPS):
        low = slots_ref[g, :256, :]
        high = slots_ref[g, 256:, :]
        out_ref[g * 256 : (g + 1) * 256, :] = jnp.where(first_half, low, high).astype(BF16)


def cross(received, blocks):
    near_re, near_im = (jnp.asarray(t, BF16) for t in near_tables())
    vmem = pl.BlockSpec(memory_space=pltpu.VMEM)
    return pl.pallas_call(
        cross_kernel,
        out_shape=jax.ShapeDtypeStruct((GROUPS * 32 * CB, 128), BF16),
        in_specs=[vmem, pl.BlockSpec(memory_space=pltpu.SMEM), vmem, vmem],
        out_specs=vmem,
        scratch_shapes=[
            pltpu.VMEM((GROUPS * WIN * ROWS, 128), F32),
            pltpu.VMEM((512, 256), BF16),
            pltpu.VMEM((512, 256), F32),
            pltpu.VMEM((2, 512, 256), BF16),
            pltpu.VMEM((GROUPS, 4 * 256, 128), F32),
            pltpu.VMEM((GROUPS, SLOTS * 32 * CB, 128), F32),
        ],
        compiler_params=params(),
    )(received, blocks, near_re, near_im)


def lag_tables():
    shifts = np.arange(LAGS) - LAGS // 2
    angle = np.pi / F * (np.arange(PHI)[:, None] * shifts[None, :] % (2 * F))
    base = np.concatenate([np.cos(angle), np.sin(angle)], axis=1)
    high = base.astype(jnp.bfloat16)
    low = (base - high.astype(np.float64)).astype(jnp.bfloat16)
    turn = np.pi / F * (PHI * np.arange(JJ)[:, None] * shifts[None, :] % (2 * F))
    cos, sin = np.cos(turn), np.sin(turn)
    mix = np.stack([np.stack([cos, -sin], 1), np.stack([-sin, -cos], 1)], 1)
    mix = mix.reshape(JJ * 2 * 2, LAGS) / math.sqrt(F * WIN)
    return high, low, mix.astype(np.float32)


def lag_kernel(m_ref, high_ref, low_ref, mix_ref, out_ref, wide_ref, turned_ref):
    wide_ref[...] = m_ref[...].astype(F32)
    for far in range(CB):
        rows = wide_ref[pl.ds(far, PHI, stride=CB), :]
        turned_ref[far * 128 : (far + 1) * 128, :] = rows.T.astype(BF16)
    sums = jnp.dot(turned_ref[...], high_ref[...], preferred_element_type=F32)
    sums = sums + jnp.dot(turned_ref[...], low_ref[...], preferred_element_type=F32)
    for far in range(CB):
        for slot in range(SLOTS):
            total = None
            for q in range(JJ * 2):
                start = far * 128 + slot * 64 + q * CB
                rows = sums[start : start + CB]
                term = rows[:, :LAGS] * mix_ref[2 * q : 2 * q + 1, :]
                term = term + rows[:, LAGS:] * mix_ref[2 * q + 1 : 2 * q + 2, :]
                total = term if total is None else total + term
            out_ref[slot, :, far * LAGS : (far + 1) * LAGS] = total


def lags(arrived):
    high, low, mix = lag_tables()
    return pl.pallas_call(
        lag_kernel,
        out_shape=jax.ShapeDtypeStruct((SLOTS, CB, CB * LAGS), F32),
        in_specs=[pl.BlockSpec(memory_space=pltpu.VMEM)] * 4,
        out_specs=pl.BlockSpec(memory_space=pltpu.VMEM),
        scratch_shapes=[
            pltpu.VMEM((PHI * CB, 128), F32),
            pltpu.VMEM((CB * 128, PHI), BF16),
        ],
        compiler_params=params(),
    )(arrived, jnp.asarray(high), jnp.asarray(low), jnp.asarray(mix))


def local(spectra, window_valid, pair_code, block_owner):
    both = ("chan", "tm")
    tiled = spectra.reshape(CG, 2, F // 128, 128).transpose(0, 2, 1, 3).reshape(CG * F // 64, 128)
    sent = whiten(tiled, window_valid, pair_code, block_owner).reshape(PHI, ROWS, 128)
    received = lax.all_to_all(sent, both, 0, 0, tiled=True)
    blocks = received[::WIN, 2].astype(jnp.int32) * CB
    crossed = cross(received.reshape(GROUPS * WIN * ROWS, 128), blocks)
    crossed = crossed.reshape(GROUPS * 32, CB, 128)
    arrived = lax.all_to_all(crossed, both, 0, 0, tiled=True).reshape(PHI * CB, 128)
    return lags(arrived)[None]


def solution(mesh):
    return jax.shard_map(
        local,
        mesh=mesh,
        in_specs=(P("tm", "chan", None, None), P("tm"), P("chan", None), P("chan", None)),
        out_specs=P("chan", "tm", None, None),
        check_vma=False,
    )
```

```python
import math

import jax
import jax.numpy as jnp
import numpy as np
from jax import lax
from jax.experimental import pallas as pl
from jax.experimental.pallas import tpu as pltpu
from jax.sharding import PartitionSpec as P

CB = 8
G = 4
CG = G * CB
LAGS = 256
SLOTS = 2
EPS = 1e-05
GROUPS = 16
WIN = 32
BLOCKS = 32
F = 2048
JJ = 4
PHI = F // JJ
MESSAGE = JJ * 2 * CG
ROWS = 4

BF16 = jnp.bfloat16
F32 = jnp.float32


def params():
    return pltpu.CompilerParams(vmem_limit_bytes=40 << 20)


def sent_fields(code_ref, owner_ref, sent_ref):
    lane = lax.broadcasted_iota(jnp.int32, (1, 128), 1)
    fill = jnp.full((1, 128 - BLOCKS), -1, jnp.int32)
    owner = jnp.concatenate([owner_ref[...], fill], axis=1)
    code = jnp.concatenate([code_ref[...], fill], axis=1)
    rank = jnp.zeros((1, 128), jnp.int32)
    for back in range(1, BLOCKS):
        same = pltpu.roll(owner, back, 1) == owner
        rank = rank + jnp.where(same & (lane >= back), 1, 0)
    near_blk = code // 36
    far = code - near_blk * 36
    form = ((near_blk >> 1) + 2 * ((near_blk & 1) ^ rank)) * BLOCKS + lane
    place = rank * 32 + owner
    fields = jnp.where(lane < BLOCKS, far, pltpu.roll(form, BLOCKS, 1))
    fields = jnp.where(lane < 2 * BLOCKS, fields, pltpu.roll(place, 2 * BLOCKS, 1))
    fields = jnp.where(lane < 3 * BLOCKS, fields, 0)
    fields = jnp.broadcast_to(fields.astype(F32), (PHI, 128))
    sent_ref[pl.ds(2, PHI, stride=ROWS), :] = fields
    sent_ref[pl.ds(3, PHI, stride=ROWS), :] = fields


def whiten_kernel(x_ref, valid_ref, code_ref, owner_ref, out_ref, wide_ref, sent_ref):
    sent_fields(code_ref, owner_ref, sent_ref)
    wide_ref[...] = x_ref[...].astype(F32)
    tiles = F // 128
    raw = [
        [wide_ref[pl.ds(tile * 2 + part, CG, stride=tiles * 2), :] for tile in range(tiles)]
        for part in range(2)
    ]
    squares = sum(block * block for side in raw for block in side)
    mean_power = jnp.sum(squares, axis=1, keepdims=True) * (1.0 / (2 * F))
    scale = lax.rsqrt(mean_power + EPS)
    valid = jnp.broadcast_to(valid_ref[...].astype(F32), (CG, 128))
    for pair in range(JJ // 2):
        for tile in range(PHI // 128):
            rows = jnp.concatenate(
                [
                    (raw[part][j * (PHI // 128) + tile] * scale).astype(BF16).astype(F32) * valid
                    for j in (2 * pair, 2 * pair + 1)
                    for part in range(2)
                ],
                axis=0,
            )
            sent_ref[pl.ds(tile * 128 * ROWS + pair, 128, stride=ROWS), :] = rows.T
    out_ref[...] = sent_ref[...].astype(BF16)


def whiten(spectra, valid, codes, owners):
    vmem = pl.BlockSpec(memory_space=pltpu.VMEM)
    return pl.pallas_call(
        whiten_kernel,
        out_shape=jax.ShapeDtypeStruct((PHI * ROWS, 128), BF16),
        in_specs=[vmem] * 4,
        out_specs=vmem,
        scratch_shapes=[
            pltpu.VMEM((CG * F // 64, 128), F32),
            pltpu.VMEM((PHI * ROWS, 128), F32),
        ],
        compiler_params=params(),
    )(spectra, valid, codes, owners)


def near_tables():
    far_re = np.zeros((MESSAGE, 256), np.float32)
    far_im = np.zeros((MESSAGE, 256), np.float32)
    for r in range(G):
        for j in range(JJ):
            for i in range(CB):
                re_row = (j * 2) * CG + r * CB + i
                im_row = re_row + CG
                re_lane = r * 64 + (j * 2) * CB + i
                im_lane = re_lane + CB
                far_re[re_row, re_lane] = 1
                far_re[im_row, im_lane] = 1
                far_im[im_row, re_lane] = 1
                far_im[re_row, im_lane] = -1
    return far_re, far_im


def cross_kernel(
    r_ref, blocks_ref, near_re_ref, near_im_ref, out_ref, wide_ref, own_ref, far_ref, near_ref, forms_ref, slots_ref
):
    slots_ref[...] = jnp.zeros_like(slots_ref)
    wide_ref[...] = r_ref[...].astype(F32)
    quarter = lax.broadcasted_iota(jnp.int32, (32, 128), 1) // 32
    for g4 in range(GROUPS // 4):
        for q4 in range(2):
            block = wide_ref[pl.ds(g4 * 128 * ROWS + q4, 128, stride=ROWS), :]
            own_ref[g4 * 128 : (g4 + 1) * 128, q4 * 128 : (q4 + 1) * 128] = block.astype(BF16)
            turned = block.T
            for g in range(4):
                rows = None
                for q in range(4):
                    piece = turned[q * 32 : (q + 1) * 32, :]
                    shift = ((q - g) * 32) % 128
                    if shift:
                        piece = pltpu.roll(piece, shift, 1)
                    rows = piece if rows is None else jnp.where(quarter == q, piece, rows)
                start = (g4 * 4 + g) * 32
                far_ref[start : start + 32, q4 * 128 : (q4 + 1) * 128] = rows
    for part, table in enumerate((near_re_ref, near_im_ref)):
        spread = jnp.dot(own_ref[...], table[...], preferred_element_type=F32)
        near_ref[part] = spread.astype(BF16)

    lane_j = lax.broadcasted_iota(jnp.int32, (32, 256), 1) // 16 % JJ
    keeps = [jnp.where(lane_j == j, 1.0, 0.0).astype(BF16) for j in range(JJ)]

    for g in range(GROUPS):
        far_rows = [(blocks_ref[g, k] + g * CG) & (GROUPS * CG - 1) for k in range(BLOCKS)]
        far = jnp.concatenate(
            [far_ref[pl.ds(pl.multiple_of(row, CB), CB), :] for row in far_rows], axis=0
        ).astype(BF16)
        sides = [near_ref[side, g * WIN : (g + 1) * WIN, :] for side in range(2)]
        near = jnp.concatenate([side * keep for keep in keeps for side in sides], axis=0)
        cross = jnp.dot(far, near, preferred_element_type=F32)
        for half in range(2):
            rows = cross[:, half * 128 : (half + 1) * 128]
            forms_ref[g, half * 256 : (half + 1) * 256, :] = rows
            forms_ref[g, (half + 2) * 256 : (half + 3) * 256, :] = pltpu.roll(rows, 64, 1)
        for k in range(BLOCKS):
            form = pl.multiple_of(blocks_ref[g, BLOCKS + k], CB)
            place = pl.multiple_of(blocks_ref[g, 2 * BLOCKS + k], CB)
            slots_ref[g, pl.ds(place, CB), :] = forms_ref[g, pl.ds(form, CB), :]
    first_half = lax.broadcasted_iota(jnp.int32, (256, 128), 1) < 64
    for g in range(GROUPS):
        low = slots_ref[g, :256, :]
        high = slots_ref[g, 256:, :]
        out_ref[g * 256 : (g + 1) * 256, :] = jnp.where(first_half, low, high).astype(BF16)


def cross(received, blocks):
    near_re, near_im = (jnp.asarray(t, BF16) for t in near_tables())
    vmem = pl.BlockSpec(memory_space=pltpu.VMEM)
    return pl.pallas_call(
        cross_kernel,
        out_shape=jax.ShapeDtypeStruct((GROUPS * 32 * CB, 128), BF16),
        in_specs=[vmem, pl.BlockSpec(memory_space=pltpu.SMEM), vmem, vmem],
        out_specs=vmem,
        scratch_shapes=[
            pltpu.VMEM((GROUPS * WIN * ROWS, 128), F32),
            pltpu.VMEM((512, 256), BF16),
            pltpu.VMEM((512, 256), F32),
            pltpu.VMEM((2, 512, 256), BF16),
            pltpu.VMEM((GROUPS, 4 * 256, 128), F32),
            pltpu.VMEM((GROUPS, SLOTS * 32 * CB, 128), F32),
        ],
        compiler_params=params(),
    )(received, blocks, near_re, near_im)


def lag_tables():
    shifts = np.arange(LAGS) - LAGS // 2
    angle = np.pi / F * (np.arange(PHI)[:, None] * shifts[None, :] % (2 * F))
    base = np.concatenate([np.cos(angle), np.sin(angle)], axis=1)
    high = base.astype(jnp.bfloat16)
    low = (base - high.astype(np.float64)).astype(jnp.bfloat16)
    turn = np.pi / F * (PHI * np.arange(JJ)[:, None] * shifts[None, :] % (2 * F))
    cos, sin = np.cos(turn), np.sin(turn)
    mix = np.stack([np.stack([cos, -sin], 1), np.stack([-sin, -cos], 1)], 1)
    mix = mix.reshape(JJ * 2 * 2, LAGS) / math.sqrt(F * WIN)
    return high, low, mix.astype(np.float32)


def lag_kernel(m_ref, high_ref, low_ref, mix_ref, out_ref, wide_ref, turned_ref):
    wide_ref[...] = m_ref[...].astype(F32)
    for far in range(CB):
        rows = wide_ref[pl.ds(far, PHI, stride=CB), :]
        turned_ref[far * 128 : (far + 1) * 128, :] = rows.T.astype(BF16)
    sums = jnp.dot(turned_ref[...], high_ref[...], preferred_element_type=F32)
    sums = sums + jnp.dot(turned_ref[...], low_ref[...], preferred_element_type=F32)
    for far in range(CB):
        for slot in range(SLOTS):
            total = None
            for q in range(JJ * 2):
                start = far * 128 + slot * 64 + q * CB
                rows = sums[start : start + CB]
                term = rows[:, :LAGS] * mix_ref[2 * q : 2 * q + 1, :]
                term = term + rows[:, LAGS:] * mix_ref[2 * q + 1 : 2 * q + 2, :]
                total = term if total is None else total + term
            out_ref[slot, :, far * LAGS : (far + 1) * LAGS] = total


def lags(arrived):
    high, low, mix = lag_tables()
    return pl.pallas_call(
        lag_kernel,
        out_shape=jax.ShapeDtypeStruct((SLOTS, CB, CB * LAGS), F32),
        in_specs=[pl.BlockSpec(memory_space=pltpu.VMEM)] * 4,
        out_specs=pl.BlockSpec(memory_space=pltpu.VMEM),
        scratch_shapes=[
            pltpu.VMEM((PHI * CB, 128), F32),
            pltpu.VMEM((CB * 128, PHI), BF16),
        ],
        compiler_params=params(),
    )(arrived, jnp.asarray(high), jnp.asarray(low), jnp.asarray(mix))


def local(spectra, window_valid, pair_code, block_owner):
    both = ("chan", "tm")
    tiled = spectra.reshape(CG, 2, F // 128, 128).transpose(0, 2, 1, 3).reshape(CG * F // 64, 128)
    sent = whiten(tiled, window_valid[None], pair_code, block_owner).reshape(PHI, ROWS, 128)
    received = lax.all_to_all(sent, both, 0, 0, tiled=True)
    blocks = received[::WIN, 2].astype(jnp.int32) * CB
    crossed = cross(received.reshape(GROUPS * WIN * ROWS, 128), blocks)
    crossed = crossed.reshape(GROUPS * 32, CB, 128)
    arrived = lax.all_to_all(crossed, both, 0, 0, tiled=True).reshape(PHI * CB, 128)
    return lags(arrived)[None]


def solution(mesh):
    return jax.shard_map(
        local,
        mesh=mesh,
        in_specs=(P("tm", "chan", None, None), P("tm"), P("chan", None), P("chan", None)),
        out_specs=P("chan", "tm", None, None),
        check_vma=False,
    )
```

```python
import math

import jax
import jax.numpy as jnp
import numpy as np
from jax import lax
from jax.experimental import pallas as pl
from jax.experimental.pallas import tpu as pltpu
from jax.sharding import PartitionSpec as P

CB = 8
G = 4
CG = G * CB
LAGS = 256
SLOTS = 2
EPS = 1e-05
GROUPS = 16
WIN = 32
BLOCKS = 32
F = 2048
JJ = 4
PHI = F // JJ
MESSAGE = JJ * 2 * CG
ROWS = 4

BF16 = jnp.bfloat16
F32 = jnp.float32


def params():
    return pltpu.CompilerParams(vmem_limit_bytes=40 << 20)


def sent_fields(code_ref, owner_ref, sent_ref):
    lane = lax.broadcasted_iota(jnp.int32, (1, 128), 1)
    fill = jnp.full((1, 128 - BLOCKS), -1, jnp.int32)
    owner = jnp.concatenate([owner_ref[...], fill], axis=1)
    code = jnp.concatenate([code_ref[...], fill], axis=1)
    rank = jnp.zeros((1, 128), jnp.int32)
    for back in range(1, BLOCKS):
        same = pltpu.roll(owner, back, 1) == owner
        rank = rank + jnp.where(same & (lane >= back), 1, 0)
    near_blk = code // 36
    far = code - near_blk * 36
    form = ((near_blk >> 1) + 2 * ((near_blk & 1) ^ rank)) * BLOCKS + lane
    place = rank * 32 + owner
    fields = jnp.where(lane < BLOCKS, far, pltpu.roll(form, BLOCKS, 1))
    fields = jnp.where(lane < 2 * BLOCKS, fields, pltpu.roll(place, 2 * BLOCKS, 1))
    fields = jnp.where(lane < 3 * BLOCKS, fields, 0)
    fields = jnp.broadcast_to(fields.astype(F32), (PHI, 128))
    sent_ref[pl.ds(2, PHI, stride=ROWS), :] = fields
    sent_ref[pl.ds(3, PHI, stride=ROWS), :] = fields


def whiten_kernel(x_ref, valid_ref, code_ref, owner_ref, out_ref, wide_ref, sent_ref):
    sent_fields(code_ref, owner_ref, sent_ref)
    wide_ref[...] = x_ref[...].astype(F32)
    tiles = F // 128
    raw = [
        [wide_ref[pl.ds(tile * 2 + part, CG, stride=tiles * 2), :] for tile in range(tiles)]
        for part in range(2)
    ]
    squares = sum(block * block for side in raw for block in side)
    mean_power = jnp.sum(squares, axis=1, keepdims=True) * (1.0 / (2 * F))
    scale = lax.rsqrt(mean_power + EPS)
    valid = valid_ref[0].astype(F32)
    for pair in range(JJ // 2):
        for tile in range(PHI // 128):
            rows = jnp.concatenate(
                [
                    (raw[part][j * (PHI // 128) + tile] * scale).astype(BF16).astype(F32) * valid
                    for j in (2 * pair, 2 * pair + 1)
                    for part in range(2)
                ],
                axis=0,
            )
            sent_ref[pl.ds(tile * 128 * ROWS + pair, 128, stride=ROWS), :] = rows.T
    out_ref[...] = sent_ref[...].astype(BF16)


def whiten(spectra, valid, codes, owners):
    vmem = pl.BlockSpec(memory_space=pltpu.VMEM)
    return pl.pallas_call(
        whiten_kernel,
        out_shape=jax.ShapeDtypeStruct((PHI * ROWS, 128), BF16),
        in_specs=[vmem, pl.BlockSpec(memory_space=pltpu.SMEM), vmem, vmem],
        out_specs=vmem,
        scratch_shapes=[
            pltpu.VMEM((CG * F // 64, 128), F32),
            pltpu.VMEM((PHI * ROWS, 128), F32),
        ],
        compiler_params=params(),
    )(spectra, valid, codes, owners)


def near_tables():
    far_re = np.zeros((MESSAGE, 256), np.float32)
    far_im = np.zeros((MESSAGE, 256), np.float32)
    for r in range(G):
        for j in range(JJ):
            for i in range(CB):
                re_row = (j * 2) * CG + r * CB + i
                im_row = re_row + CG
                re_lane = r * 64 + (j * 2) * CB + i
                im_lane = re_lane + CB
                far_re[re_row, re_lane] = 1
                far_re[im_row, im_lane] = 1
                far_im[im_row, re_lane] = 1
                far_im[re_row, im_lane] = -1
    return far_re, far_im


def cross_kernel(
    r_ref, blocks_ref, near_re_ref, near_im_ref, out_ref, wide_ref, own_ref, far_ref, near_ref, forms_ref, slots_ref
):
    slots_ref[...] = jnp.zeros_like(slots_ref)
    wide_ref[...] = r_ref[...].astype(F32)
    quarter = lax.broadcasted_iota(jnp.int32, (32, 128), 1) // 32
    for g4 in range(GROUPS // 4):
        for q4 in range(2):
            block = wide_ref[pl.ds(g4 * 128 * ROWS + q4, 128, stride=ROWS), :]
            own_ref[g4 * 128 : (g4 + 1) * 128, q4 * 128 : (q4 + 1) * 128] = block.astype(BF16)
            turned = block.T
            for g in range(4):
                rows = None
                for q in range(4):
                    piece = turned[q * 32 : (q + 1) * 32, :]
                    shift = ((q - g) * 32) % 128
                    if shift:
                        piece = pltpu.roll(piece, shift, 1)
                    rows = piece if rows is None else jnp.where(quarter == q, piece, rows)
                start = (g4 * 4 + g) * 32
                far_ref[start : start + 32, q4 * 128 : (q4 + 1) * 128] = rows
    for part, table in enumerate((near_re_ref, near_im_ref)):
        spread = jnp.dot(own_ref[...], table[...], preferred_element_type=F32)
        near_ref[part] = spread.astype(BF16)

    lane_j = lax.broadcasted_iota(jnp.int32, (32, 256), 1) // 16 % JJ
    keeps = [jnp.where(lane_j == j, 1.0, 0.0).astype(BF16) for j in range(JJ)]

    for g in range(GROUPS):
        far_rows = [blocks_ref[g, k] for k in range(BLOCKS)]
        far = jnp.concatenate(
            [far_ref[pl.ds(pl.multiple_of(row, CB), CB), :] for row in far_rows], axis=0
        ).astype(BF16)
        sides = [near_ref[side, g * WIN : (g + 1) * WIN, :] for side in range(2)]
        near = jnp.concatenate([side * keep for keep in keeps for side in sides], axis=0)
        cross = jnp.dot(far, near, preferred_element_type=F32)
        for half in range(2):
            rows = cross[:, half * 128 : (half + 1) * 128]
            forms_ref[g, half * 256 : (half + 1) * 256, :] = rows
            forms_ref[g, (half + 2) * 256 : (half + 3) * 256, :] = pltpu.roll(rows, 64, 1)
        for k in range(BLOCKS):
            form = pl.multiple_of(blocks_ref[g, BLOCKS + k], CB)
            place = pl.multiple_of(blocks_ref[g, 2 * BLOCKS + k], CB)
            slots_ref[g, pl.ds(place, CB), :] = forms_ref[g, pl.ds(form, CB), :]
    first_half = lax.broadcasted_iota(jnp.int32, (256, 128), 1) < 64
    for g in range(GROUPS):
        low = slots_ref[g, :256, :]
        high = slots_ref[g, 256:, :]
        out_ref[g * 256 : (g + 1) * 256, :] = jnp.where(first_half, low, high).astype(BF16)


def cross(received, blocks):
    near_re, near_im = (jnp.asarray(t, BF16) for t in near_tables())
    vmem = pl.BlockSpec(memory_space=pltpu.VMEM)
    return pl.pallas_call(
        cross_kernel,
        out_shape=jax.ShapeDtypeStruct((GROUPS * 32 * CB, 128), BF16),
        in_specs=[vmem, pl.BlockSpec(memory_space=pltpu.SMEM), vmem, vmem],
        out_specs=vmem,
        scratch_shapes=[
            pltpu.VMEM((GROUPS * WIN * ROWS, 128), F32),
            pltpu.VMEM((512, 256), BF16),
            pltpu.VMEM((512, 256), F32),
            pltpu.VMEM((2, 512, 256), BF16),
            pltpu.VMEM((GROUPS, 4 * 256, 128), F32),
            pltpu.VMEM((GROUPS, SLOTS * 32 * CB, 128), F32),
        ],
        compiler_params=params(),
    )(received, blocks, near_re, near_im)


def lag_tables():
    shifts = np.arange(LAGS) - LAGS // 2
    angle = np.pi / F * (np.arange(PHI)[:, None] * shifts[None, :] % (2 * F))
    base = np.concatenate([np.cos(angle), np.sin(angle)], axis=1)
    high = base.astype(jnp.bfloat16)
    low = (base - high.astype(np.float64)).astype(jnp.bfloat16)
    turn = np.pi / F * (PHI * np.arange(JJ)[:, None] * shifts[None, :] % (2 * F))
    cos, sin = np.cos(turn), np.sin(turn)
    mix = np.stack([np.stack([cos, -sin], 1), np.stack([-sin, -cos], 1)], 1)
    mix = mix.reshape(JJ * 2 * 2, LAGS) / math.sqrt(F * WIN)
    return high, low, mix.astype(np.float32)


def lag_kernel(m_ref, high_ref, low_ref, mix_ref, out_ref, wide_ref, turned_ref):
    wide_ref[...] = m_ref[...].astype(F32)
    for far in range(CB):
        rows = wide_ref[pl.ds(far, PHI, stride=CB), :]
        turned_ref[far * 128 : (far + 1) * 128, :] = rows.T.astype(BF16)
    sums = jnp.dot(turned_ref[...], high_ref[...], preferred_element_type=F32)
    sums = sums + jnp.dot(turned_ref[...], low_ref[...], preferred_element_type=F32)
    for far in range(CB):
        for slot in range(SLOTS):
            total = None
            for q in range(JJ * 2):
                start = far * 128 + slot * 64 + q * CB
                rows = sums[start : start + CB]
                term = rows[:, :LAGS] * mix_ref[2 * q : 2 * q + 1, :]
                term = term + rows[:, LAGS:] * mix_ref[2 * q + 1 : 2 * q + 2, :]
                total = term if total is None else total + term
            out_ref[slot, :, far * LAGS : (far + 1) * LAGS] = total


def lags(arrived):
    high, low, mix = lag_tables()
    return pl.pallas_call(
        lag_kernel,
        out_shape=jax.ShapeDtypeStruct((SLOTS, CB, CB * LAGS), F32),
        in_specs=[pl.BlockSpec(memory_space=pltpu.VMEM)] * 4,
        out_specs=pl.BlockSpec(memory_space=pltpu.VMEM),
        scratch_shapes=[
            pltpu.VMEM((PHI * CB, 128), F32),
            pltpu.VMEM((CB * 128, PHI), BF16),
        ],
        compiler_params=params(),
    )(arrived, jnp.asarray(high), jnp.asarray(low), jnp.asarray(mix))


def local(spectra, window_valid, pair_code, block_owner):
    both = ("chan", "tm")
    tiled = spectra.reshape(CG, 2, F // 128, 128).transpose(0, 2, 1, 3).reshape(CG * F // 64, 128)
    sent = whiten(tiled, window_valid, pair_code, block_owner).reshape(PHI, ROWS, 128)
    received = lax.all_to_all(sent, both, 0, 0, tiled=True)
    blocks = received[::WIN, 2].astype(jnp.int32) * CB
    group = jnp.arange(GROUPS, dtype=jnp.int32)[:, None]
    far = (blocks + group * CG) & (GROUPS * CG - 1)
    blocks = jnp.where(jnp.arange(128)[None, :] < BLOCKS, far, blocks)
    crossed = cross(received.reshape(GROUPS * WIN * ROWS, 128), blocks)
    crossed = crossed.reshape(GROUPS * 32, CB, 128)
    arrived = lax.all_to_all(crossed, both, 0, 0, tiled=True).reshape(PHI * CB, 128)
    return lags(arrived)[None]


def solution(mesh):
    return jax.shard_map(
        local,
        mesh=mesh,
        in_specs=(P("tm", "chan", None, None), P("tm"), P("chan", None), P("chan", None)),
        out_specs=P("chan", "tm", None, None),
        check_vma=False,
    )
```

```python
import math

import jax
import jax.numpy as jnp
import numpy as np
from jax import lax
from jax.experimental import pallas as pl
from jax.experimental.pallas import tpu as pltpu
from jax.sharding import PartitionSpec as P

CB = 8
G = 4
CG = G * CB
LAGS = 256
SLOTS = 2
EPS = 1e-05
GROUPS = 16
WIN = 32
BLOCKS = 32
F = 2048
JJ = 4
PHI = F // JJ
MESSAGE = JJ * 2 * CG
ROWS = 4

BF16 = jnp.bfloat16
F32 = jnp.float32


def params():
    return pltpu.CompilerParams(vmem_limit_bytes=40 << 20)


def sent_fields(code_ref, owner_ref, sent_ref):
    lane = lax.broadcasted_iota(jnp.int32, (1, 128), 1)
    fill = jnp.full((1, 128 - BLOCKS), -1, jnp.int32)
    owner = jnp.concatenate([owner_ref[...], fill], axis=1)
    code = jnp.concatenate([code_ref[...], fill], axis=1)
    rank = jnp.zeros((1, 128), jnp.int32)
    for back in range(1, BLOCKS):
        same = pltpu.roll(owner, back, 1) == owner
        rank = rank + jnp.where(same & (lane >= back), 1, 0)
    near_blk = code // 36
    far = code - near_blk * 36
    form = ((near_blk >> 1) + 2 * ((near_blk & 1) ^ rank)) * BLOCKS + lane
    place = rank * 32 + owner
    fields = jnp.where(lane < BLOCKS, far, pltpu.roll(form, BLOCKS, 1))
    fields = jnp.where(lane < 2 * BLOCKS, fields, pltpu.roll(place, 2 * BLOCKS, 1))
    fields = jnp.where(lane < 3 * BLOCKS, fields, 0)
    fields = jnp.broadcast_to(fields.astype(F32), (PHI, 128))
    sent_ref[pl.ds(2, PHI, stride=ROWS), :] = fields
    sent_ref[pl.ds(3, PHI, stride=ROWS), :] = fields


def whiten_kernel(wide_ref, valid_ref, code_ref, owner_ref, out_ref, sent_ref):
    sent_fields(code_ref, owner_ref, sent_ref)
    tiles = F // 128
    raw = [
        [wide_ref[pl.ds(tile * 2 + part, CG, stride=tiles * 2), :] for tile in range(tiles)]
        for part in range(2)
    ]
    squares = sum(block * block for side in raw for block in side)
    mean_power = jnp.sum(squares, axis=1, keepdims=True) * (1.0 / (2 * F))
    scale = lax.rsqrt(mean_power + EPS)
    valid = valid_ref[0].astype(F32)
    for pair in range(JJ // 2):
        for tile in range(PHI // 128):
            rows = jnp.concatenate(
                [
                    (raw[part][j * (PHI // 128) + tile] * scale).astype(BF16).astype(F32) * valid
                    for j in (2 * pair, 2 * pair + 1)
                    for part in range(2)
                ],
                axis=0,
            )
            sent_ref[pl.ds(tile * 128 * ROWS + pair, 128, stride=ROWS), :] = rows.T
    out_ref[...] = sent_ref[...].astype(BF16)


def whiten(spectra, valid, codes, owners):
    vmem = pl.BlockSpec(memory_space=pltpu.VMEM)
    return pl.pallas_call(
        whiten_kernel,
        out_shape=jax.ShapeDtypeStruct((PHI * ROWS, 128), BF16),
        in_specs=[vmem, pl.BlockSpec(memory_space=pltpu.SMEM), vmem, vmem],
        out_specs=vmem,
        scratch_shapes=[
            pltpu.VMEM((PHI * ROWS, 128), F32),
        ],
        compiler_params=params(),
    )(spectra, valid, codes, owners)


def near_tables():
    far_re = np.zeros((MESSAGE, 256), np.float32)
    far_im = np.zeros((MESSAGE, 256), np.float32)
    for r in range(G):
        for j in range(JJ):
            for i in range(CB):
                re_row = (j * 2) * CG + r * CB + i
                im_row = re_row + CG
                re_lane = r * 64 + (j * 2) * CB + i
                im_lane = re_lane + CB
                far_re[re_row, re_lane] = 1
                far_re[im_row, im_lane] = 1
                far_im[im_row, re_lane] = 1
                far_im[re_row, im_lane] = -1
    return far_re, far_im


def cross_kernel(
    r_ref, blocks_ref, near_re_ref, near_im_ref, out_ref, wide_ref, own_ref, far_ref, near_ref, forms_ref, slots_ref
):
    slots_ref[...] = jnp.zeros_like(slots_ref)
    wide_ref[...] = r_ref[...].astype(F32)
    quarter = lax.broadcasted_iota(jnp.int32, (32, 128), 1) // 32
    for g4 in range(GROUPS // 4):
        for q4 in range(2):
            block = wide_ref[pl.ds(g4 * 128 * ROWS + q4, 128, stride=ROWS), :]
            own_ref[g4 * 128 : (g4 + 1) * 128, q4 * 128 : (q4 + 1) * 128] = block.astype(BF16)
            turned = block.T
            for g in range(4):
                rows = None
                for q in range(4):
                    piece = turned[q * 32 : (q + 1) * 32, :]
                    shift = ((q - g) * 32) % 128
                    if shift:
                        piece = pltpu.roll(piece, shift, 1)
                    rows = piece if rows is None else jnp.where(quarter == q, piece, rows)
                start = (g4 * 4 + g) * 32
                far_ref[start : start + 32, q4 * 128 : (q4 + 1) * 128] = rows
    for part, table in enumerate((near_re_ref, near_im_ref)):
        spread = jnp.dot(own_ref[...], table[...], preferred_element_type=F32)
        near_ref[part] = spread.astype(BF16)

    lane_j = lax.broadcasted_iota(jnp.int32, (32, 256), 1) // 16 % JJ
    keeps = [jnp.where(lane_j == j, 1.0, 0.0).astype(BF16) for j in range(JJ)]

    for g in range(GROUPS):
        far_rows = [(blocks_ref[g, k] + g * CG) & (GROUPS * CG - 1) for k in range(BLOCKS)]
        far = jnp.concatenate(
            [far_ref[pl.ds(pl.multiple_of(row, CB), CB), :] for row in far_rows], axis=0
        ).astype(BF16)
        sides = [near_ref[side, g * WIN : (g + 1) * WIN, :] for side in range(2)]
        near = jnp.concatenate([side * keep for keep in keeps for side in sides], axis=0)
        cross = jnp.dot(far, near, preferred_element_type=F32)
        for half in range(2):
            rows = cross[:, half * 128 : (half + 1) * 128]
            forms_ref[g, half * 256 : (half + 1) * 256, :] = rows
            forms_ref[g, (half + 2) * 256 : (half + 3) * 256, :] = pltpu.roll(rows, 64, 1)
        for k in range(BLOCKS):
            form = pl.multiple_of(blocks_ref[g, BLOCKS + k], CB)
            place = pl.multiple_of(blocks_ref[g, 2 * BLOCKS + k], CB)
            slots_ref[g, pl.ds(place, CB), :] = forms_ref[g, pl.ds(form, CB), :]
    first_half = lax.broadcasted_iota(jnp.int32, (256, 128), 1) < 64
    for g in range(GROUPS):
        low = slots_ref[g, :256, :]
        high = slots_ref[g, 256:, :]
        out_ref[g * 256 : (g + 1) * 256, :] = jnp.where(first_half, low, high).astype(BF16)


def cross(received, blocks):
    near_re, near_im = (jnp.asarray(t, BF16) for t in near_tables())
    vmem = pl.BlockSpec(memory_space=pltpu.VMEM)
    return pl.pallas_call(
        cross_kernel,
        out_shape=jax.ShapeDtypeStruct((GROUPS * 32 * CB, 128), BF16),
        in_specs=[vmem, pl.BlockSpec(memory_space=pltpu.SMEM), vmem, vmem],
        out_specs=vmem,
        scratch_shapes=[
            pltpu.VMEM((GROUPS * WIN * ROWS, 128), F32),
            pltpu.VMEM((512, 256), BF16),
            pltpu.VMEM((512, 256), F32),
            pltpu.VMEM((2, 512, 256), BF16),
            pltpu.VMEM((GROUPS, 4 * 256, 128), F32),
            pltpu.VMEM((GROUPS, SLOTS * 32 * CB, 128), F32),
        ],
        compiler_params=params(),
    )(received, blocks, near_re, near_im)


def lag_tables():
    shifts = np.arange(LAGS) - LAGS // 2
    angle = np.pi / F * (np.arange(PHI)[:, None] * shifts[None, :] % (2 * F))
    base = np.concatenate([np.cos(angle), np.sin(angle)], axis=1)
    high = base.astype(jnp.bfloat16)
    low = (base - high.astype(np.float64)).astype(jnp.bfloat16)
    turn = np.pi / F * (PHI * np.arange(JJ)[:, None] * shifts[None, :] % (2 * F))
    cos, sin = np.cos(turn), np.sin(turn)
    mix = np.stack([np.stack([cos, -sin], 1), np.stack([-sin, -cos], 1)], 1)
    mix = mix.reshape(JJ * 2 * 2, LAGS) / math.sqrt(F * WIN)
    return high, low, mix.astype(np.float32)


def lag_kernel(m_ref, high_ref, low_ref, mix_ref, out_ref, wide_ref, turned_ref):
    wide_ref[...] = m_ref[...].astype(F32)
    for far2 in range(CB // 2):
        rows = jnp.concatenate(
            [wide_ref[pl.ds(far2 * 2 + half, PHI, stride=CB), :].T for half in range(2)], axis=0
        ).astype(BF16)
        sums = jnp.dot(rows, high_ref[...], preferred_element_type=F32)
        sums = sums + jnp.dot(rows, low_ref[...], preferred_element_type=F32)
        for half in range(2):
            far = far2 * 2 + half
            for slot in range(SLOTS):
                total = None
                for q in range(JJ * 2):
                    start = half * 128 + slot * 64 + q * CB
                    rows_q = sums[start : start + CB]
                    term = rows_q[:, :LAGS] * mix_ref[2 * q : 2 * q + 1, :]
                    term = term + rows_q[:, LAGS:] * mix_ref[2 * q + 1 : 2 * q + 2, :]
                    total = term if total is None else total + term
                out_ref[slot, :, far * LAGS : (far + 1) * LAGS] = total


def lags(arrived):
    high, low, mix = lag_tables()
    return pl.pallas_call(
        lag_kernel,
        out_shape=jax.ShapeDtypeStruct((SLOTS, CB, CB * LAGS), F32),
        in_specs=[pl.BlockSpec(memory_space=pltpu.VMEM)] * 4,
        out_specs=pl.BlockSpec(memory_space=pltpu.VMEM),
        scratch_shapes=[
            pltpu.VMEM((PHI * CB, 128), F32),
            pltpu.VMEM((CB * 128, PHI), BF16),
        ],
        compiler_params=params(),
    )(arrived, jnp.asarray(high), jnp.asarray(low), jnp.asarray(mix))


def local(spectra, window_valid, pair_code, block_owner):
    both = ("chan", "tm")
    tiled = spectra.astype(F32).reshape(CG, 2, F // 128, 128).transpose(0, 2, 1, 3).reshape(CG * F // 64, 128)
    sent = whiten(tiled, window_valid, pair_code, block_owner).reshape(PHI, ROWS, 128)
    received = lax.all_to_all(sent, both, 0, 0, tiled=True)
    blocks = received[::WIN, 2].astype(jnp.int32) * CB
    crossed = cross(received.reshape(GROUPS * WIN * ROWS, 128), blocks)
    crossed = crossed.reshape(GROUPS * 32, CB, 128)
    arrived = lax.all_to_all(crossed, both, 0, 0, tiled=True).reshape(PHI * CB, 128)
    return lags(arrived)[None]


def solution(mesh):
    return jax.shard_map(
        local,
        mesh=mesh,
        in_specs=(P("tm", "chan", None, None), P("tm"), P("chan", None), P("chan", None)),
        out_specs=P("chan", "tm", None, None),
        check_vma=False,
    )
```

```python
import math

import jax
import jax.numpy as jnp
import numpy as np
from jax import lax
from jax.experimental import pallas as pl
from jax.experimental.pallas import tpu as pltpu
from jax.sharding import PartitionSpec as P

CB = 8
G = 4
CG = G * CB
LAGS = 256
SLOTS = 2
EPS = 1e-05
GROUPS = 16
WIN = 32
BLOCKS = 32
F = 2048
JJ = 4
PHI = F // JJ
MESSAGE = JJ * 2 * CG
ROWS = 4

BF16 = jnp.bfloat16
F32 = jnp.float32


def params():
    return pltpu.CompilerParams(vmem_limit_bytes=40 << 20)


def fields_kernel(code_ref, owner_ref, out_ref):
    lane = lax.broadcasted_iota(jnp.int32, (1, 128), 1)
    fill = jnp.full((1, 128 - BLOCKS), -1, jnp.int32)
    owner = jnp.concatenate([owner_ref[...], fill], axis=1)
    code = jnp.concatenate([code_ref[...], fill], axis=1)
    rank = jnp.zeros((1, 128), jnp.int32)
    for back in range(1, BLOCKS):
        same = pltpu.roll(owner, back, 1) == owner
        rank = rank + jnp.where(same & (lane >= back), 1, 0)
    near_blk = code // 36
    far = code - near_blk * 36
    form = ((near_blk >> 1) + 2 * ((near_blk & 1) ^ rank)) * BLOCKS + lane
    place = rank * 32 + owner
    fields = jnp.where(lane < BLOCKS, far, pltpu.roll(form, BLOCKS, 1))
    fields = jnp.where(lane < 2 * BLOCKS, fields, pltpu.roll(place, 2 * BLOCKS, 1))
    fields = jnp.where(lane < 3 * BLOCKS, fields, 0)
    out_ref[...] = fields.astype(F32)


def whiten_kernel(x_ref, valid_ref, fields_ref, out_ref, wide_ref, sent_ref):
    fields = jnp.broadcast_to(fields_ref[...], (PHI, 128))
    sent_ref[pl.ds(2, PHI, stride=ROWS), :] = fields
    sent_ref[pl.ds(3, PHI, stride=ROWS), :] = fields
    wide_ref[...] = x_ref[...].astype(F32)
    tiles = F // 128
    raw = [
        [wide_ref[pl.ds(tile * 2 + part, CG, stride=tiles * 2), :] for tile in range(tiles)]
        for part in range(2)
    ]
    squares = sum(block * block for side in raw for block in side)
    mean_power = jnp.sum(squares, axis=1, keepdims=True) * (1.0 / (2 * F))
    scale = lax.rsqrt(mean_power + EPS)
    valid = valid_ref[0].astype(F32)
    for pair in range(JJ // 2):
        for tile in range(PHI // 128):
            rows = jnp.concatenate(
                [
                    (raw[part][j * (PHI // 128) + tile] * scale).astype(BF16).astype(F32) * valid
                    for j in (2 * pair, 2 * pair + 1)
                    for part in range(2)
                ],
                axis=0,
            )
            sent_ref[pl.ds(tile * 128 * ROWS + pair, 128, stride=ROWS), :] = rows.T
    out_ref[...] = sent_ref[...].astype(BF16)


def whiten(spectra, valid, codes, owners):
    vmem = pl.BlockSpec(memory_space=pltpu.VMEM)
    fields = pl.pallas_call(
        fields_kernel,
        out_shape=jax.ShapeDtypeStruct((1, 128), F32),
        in_specs=[vmem] * 2,
        out_specs=vmem,
        compiler_params=params(),
        cost_estimate=pl.CostEstimate(flops=1 << 22, bytes_accessed=1 << 20, transcendentals=0),
    )(codes, owners)
    return pl.pallas_call(
        whiten_kernel,
        out_shape=jax.ShapeDtypeStruct((PHI * ROWS, 128), BF16),
        in_specs=[vmem, pl.BlockSpec(memory_space=pltpu.SMEM), vmem],
        out_specs=vmem,
        scratch_shapes=[
            pltpu.VMEM((CG * F // 64, 128), F32),
            pltpu.VMEM((PHI * ROWS, 128), F32),
        ],
        compiler_params=params(),
    )(spectra, valid, fields)


def near_tables():
    far_re = np.zeros((MESSAGE, 256), np.float32)
    far_im = np.zeros((MESSAGE, 256), np.float32)
    for r in range(G):
        for j in range(JJ):
            for i in range(CB):
                re_row = (j * 2) * CG + r * CB + i
                im_row = re_row + CG
                re_lane = r * 64 + (j * 2) * CB + i
                im_lane = re_lane + CB
                far_re[re_row, re_lane] = 1
                far_re[im_row, im_lane] = 1
                far_im[im_row, re_lane] = 1
                far_im[re_row, im_lane] = -1
    return far_re, far_im


def cross_kernel(
    r_ref, blocks_ref, near_re_ref, near_im_ref, out_ref, wide_ref, own_ref, far_ref, near_ref, forms_ref, slots_ref
):
    slots_ref[...] = jnp.zeros_like(slots_ref)
    wide_ref[...] = r_ref[...].astype(F32)
    quarter = lax.broadcasted_iota(jnp.int32, (32, 128), 1) // 32
    for g4 in range(GROUPS // 4):
        for q4 in range(2):
            block = wide_ref[pl.ds(g4 * 128 * ROWS + q4, 128, stride=ROWS), :]
            own_ref[g4 * 128 : (g4 + 1) * 128, q4 * 128 : (q4 + 1) * 128] = block.astype(BF16)
            turned = block.T
            for g in range(4):
                rows = None
                for q in range(4):
                    piece = turned[q * 32 : (q + 1) * 32, :]
                    shift = ((q - g) * 32) % 128
                    if shift:
                        piece = pltpu.roll(piece, shift, 1)
                    rows = piece if rows is None else jnp.where(quarter == q, piece, rows)
                start = (g4 * 4 + g) * 32
                far_ref[start : start + 32, q4 * 128 : (q4 + 1) * 128] = rows
    for part, table in enumerate((near_re_ref, near_im_ref)):
        spread = jnp.dot(own_ref[...], table[...], preferred_element_type=F32)
        near_ref[part] = spread.astype(BF16)

    lane_j = lax.broadcasted_iota(jnp.int32, (32, 256), 1) // 16 % JJ
    keeps = [jnp.where(lane_j == j, 1.0, 0.0).astype(BF16) for j in range(JJ)]

    for g in range(GROUPS):
        far_rows = [(blocks_ref[g, k] + g * CG) & (GROUPS * CG - 1) for k in range(BLOCKS)]
        far = jnp.concatenate(
            [far_ref[pl.ds(pl.multiple_of(row, CB), CB), :] for row in far_rows], axis=0
        ).astype(BF16)
        sides = [near_ref[side, g * WIN : (g + 1) * WIN, :] for side in range(2)]
        near = jnp.concatenate([side * keep for keep in keeps for side in sides], axis=0)
        cross = jnp.dot(far, near, preferred_element_type=F32)
        for half in range(2):
            rows = cross[:, half * 128 : (half + 1) * 128]
            forms_ref[g, half * 256 : (half + 1) * 256, :] = rows
            forms_ref[g, (half + 2) * 256 : (half + 3) * 256, :] = pltpu.roll(rows, 64, 1)
        for k in range(BLOCKS):
            form = pl.multiple_of(blocks_ref[g, BLOCKS + k], CB)
            place = pl.multiple_of(blocks_ref[g, 2 * BLOCKS + k], CB)
            slots_ref[g, pl.ds(place, CB), :] = forms_ref[g, pl.ds(form, CB), :]
    first_half = lax.broadcasted_iota(jnp.int32, (256, 128), 1) < 64
    for g in range(GROUPS):
        low = slots_ref[g, :256, :]
        high = slots_ref[g, 256:, :]
        out_ref[g * 256 : (g + 1) * 256, :] = jnp.where(first_half, low, high).astype(BF16)


def cross(received, blocks):
    near_re, near_im = (jnp.asarray(t, BF16) for t in near_tables())
    vmem = pl.BlockSpec(memory_space=pltpu.VMEM)
    return pl.pallas_call(
        cross_kernel,
        out_shape=jax.ShapeDtypeStruct((GROUPS * 32 * CB, 128), BF16),
        in_specs=[vmem, pl.BlockSpec(memory_space=pltpu.SMEM), vmem, vmem],
        out_specs=vmem,
        scratch_shapes=[
            pltpu.VMEM((GROUPS * WIN * ROWS, 128), F32),
            pltpu.VMEM((512, 256), BF16),
            pltpu.VMEM((512, 256), F32),
            pltpu.VMEM((2, 512, 256), BF16),
            pltpu.VMEM((GROUPS, 4 * 256, 128), F32),
            pltpu.VMEM((GROUPS, SLOTS * 32 * CB, 128), F32),
        ],
        compiler_params=params(),
    )(received, blocks, near_re, near_im)


def lag_tables():
    shifts = np.arange(LAGS) - LAGS // 2
    angle = np.pi / F * (np.arange(PHI)[:, None] * shifts[None, :] % (2 * F))
    base = np.concatenate([np.cos(angle), np.sin(angle)], axis=1)
    high = base.astype(jnp.bfloat16)
    low = (base - high.astype(np.float64)).astype(jnp.bfloat16)
    turn = np.pi / F * (PHI * np.arange(JJ)[:, None] * shifts[None, :] % (2 * F))
    cos, sin = np.cos(turn), np.sin(turn)
    mix = np.stack([np.stack([cos, -sin], 1), np.stack([-sin, -cos], 1)], 1)
    mix = mix.reshape(JJ * 2 * 2, LAGS) / math.sqrt(F * WIN)
    return high, low, mix.astype(np.float32)


def lag_kernel(m_ref, high_ref, low_ref, mix_ref, out_ref, wide_ref, turned_ref):
    wide_ref[...] = m_ref[...].astype(F32)
    for far in range(CB):
        rows = wide_ref[pl.ds(far, PHI, stride=CB), :]
        turned_ref[far * 128 : (far + 1) * 128, :] = rows.T.astype(BF16)
    sums = jnp.dot(turned_ref[...], high_ref[...], preferred_element_type=F32)
    sums = sums + jnp.dot(turned_ref[...], low_ref[...], preferred_element_type=F32)
    for far in range(CB):
        for slot in range(SLOTS):
            total = None
            for q in range(JJ * 2):
                start = far * 128 + slot * 64 + q * CB
                rows = sums[start : start + CB]
                term = rows[:, :LAGS] * mix_ref[2 * q : 2 * q + 1, :]
                term = term + rows[:, LAGS:] * mix_ref[2 * q + 1 : 2 * q + 2, :]
                total = term if total is None else total + term
            out_ref[slot, :, far * LAGS : (far + 1) * LAGS] = total


def lags(arrived):
    high, low, mix = lag_tables()
    return pl.pallas_call(
        lag_kernel,
        out_shape=jax.ShapeDtypeStruct((SLOTS, CB, CB * LAGS), F32),
        in_specs=[pl.BlockSpec(memory_space=pltpu.VMEM)] * 4,
        out_specs=pl.BlockSpec(memory_space=pltpu.VMEM),
        scratch_shapes=[
            pltpu.VMEM((PHI * CB, 128), F32),
            pltpu.VMEM((CB * 128, PHI), BF16),
        ],
        compiler_params=params(),
    )(arrived, jnp.asarray(high), jnp.asarray(low), jnp.asarray(mix))


def local(spectra, window_valid, pair_code, block_owner):
    both = ("chan", "tm")
    tiled = spectra.reshape(CG, 2, F // 128, 128).transpose(0, 2, 1, 3).reshape(CG * F // 64, 128)
    sent = whiten(tiled, window_valid, pair_code, block_owner).reshape(PHI, ROWS, 128)
    received = lax.all_to_all(sent, both, 0, 0, tiled=True)
    blocks = received[::WIN, 2].astype(jnp.int32) * CB
    crossed = cross(received.reshape(GROUPS * WIN * ROWS, 128), blocks)
    crossed = crossed.reshape(GROUPS * 32, CB, 128)
    arrived = lax.all_to_all(crossed, both, 0, 0, tiled=True).reshape(PHI * CB, 128)
    return lags(arrived)[None]


def solution(mesh):
    return jax.shard_map(
        local,
        mesh=mesh,
        in_specs=(P("tm", "chan", None, None), P("tm"), P("chan", None), P("chan", None)),
        out_specs=P("chan", "tm", None, None),
        check_vma=False,
    )
```

```python
import math

import jax
import jax.numpy as jnp
import numpy as np
from jax import lax
from jax.experimental import pallas as pl
from jax.experimental.pallas import tpu as pltpu
from jax.sharding import PartitionSpec as P

CB = 8
G = 4
CG = G * CB
LAGS = 256
SLOTS = 2
EPS = 1e-05
GROUPS = 16
WIN = 32
BLOCKS = 32
F = 2048
JJ = 4
PHI = F // JJ
MESSAGE = JJ * 2 * CG
ROWS = 4

BF16 = jnp.bfloat16
F32 = jnp.float32


def params():
    return pltpu.CompilerParams(vmem_limit_bytes=40 << 20)


def fields_kernel(code_ref, owner_ref, out_ref):
    lane = lax.broadcasted_iota(jnp.int32, (1, 128), 1)
    fill = jnp.full((1, 128 - BLOCKS), -1, jnp.int32)
    owner = jnp.concatenate([owner_ref[...], fill], axis=1)
    code = jnp.concatenate([code_ref[...], fill], axis=1)
    rank = jnp.zeros((1, 128), jnp.int32)
    for back in range(1, BLOCKS):
        same = pltpu.roll(owner, back, 1) == owner
        rank = rank + jnp.where(same & (lane >= back), 1, 0)
    near_blk = code // 36
    far = code - near_blk * 36
    form = ((near_blk >> 1) + 2 * ((near_blk & 1) ^ rank)) * BLOCKS + lane
    place = rank * 32 + owner
    fields = jnp.where(lane < BLOCKS, far, pltpu.roll(form, BLOCKS, 1))
    fields = jnp.where(lane < 2 * BLOCKS, fields, pltpu.roll(place, 2 * BLOCKS, 1))
    fields = jnp.where(lane < 3 * BLOCKS, fields, 0)
    out_ref[...] = fields.astype(F32)


def whiten_kernel(x_ref, valid_ref, fields_ref, out_ref, wide_ref, sent_ref):
    fields = jnp.broadcast_to(fields_ref[...], (PHI, 128))
    sent_ref[pl.ds(2, PHI, stride=ROWS), :] = fields
    sent_ref[pl.ds(3, PHI, stride=ROWS), :] = fields
    wide_ref[...] = x_ref[...].astype(F32)
    tiles = F // 128
    raw = [
        [wide_ref[pl.ds(tile * 2 + part, CG, stride=tiles * 2), :] for tile in range(tiles)]
        for part in range(2)
    ]
    squares = sum(block * block for side in raw for block in side)
    mean_power = jnp.sum(squares, axis=1, keepdims=True) * (1.0 / (2 * F))
    scale = lax.rsqrt(mean_power + EPS)
    valid = valid_ref[0].astype(F32)
    for pair in range(JJ // 2):
        for tile in range(PHI // 128):
            rows = jnp.concatenate(
                [
                    (raw[part][j * (PHI // 128) + tile] * scale).astype(BF16).astype(F32) * valid
                    for j in (2 * pair, 2 * pair + 1)
                    for part in range(2)
                ],
                axis=0,
            )
            sent_ref[pl.ds(tile * 128 * ROWS + pair, 128, stride=ROWS), :] = rows.T
    out_ref[...] = sent_ref[...].astype(BF16)


def whiten(spectra, valid, codes, owners):
    vmem = pl.BlockSpec(memory_space=pltpu.VMEM)
    fields = pl.pallas_call(
        fields_kernel,
        out_shape=jax.ShapeDtypeStruct((1, 128), F32),
        in_specs=[vmem] * 2,
        out_specs=vmem,
        compiler_params=params(),
        cost_estimate=pl.CostEstimate(flops=1 << 22, bytes_accessed=1 << 20, transcendentals=0),
    )(codes, owners)
    return pl.pallas_call(
        whiten_kernel,
        out_shape=jax.ShapeDtypeStruct((PHI * ROWS, 128), BF16),
        in_specs=[vmem, pl.BlockSpec(memory_space=pltpu.SMEM), vmem],
        out_specs=vmem,
        scratch_shapes=[
            pltpu.VMEM((CG * F // 64, 128), F32),
            pltpu.VMEM((PHI * ROWS, 128), F32),
        ],
        compiler_params=params(),
    )(spectra, valid, fields)


def near_tables():
    far_re = np.zeros((MESSAGE, 256), np.float32)
    far_im = np.zeros((MESSAGE, 256), np.float32)
    for r in range(G):
        for j in range(JJ):
            for i in range(CB):
                re_row = (j * 2) * CG + r * CB + i
                im_row = re_row + CG
                re_lane = r * 64 + (j * 2) * CB + i
                im_lane = re_lane + CB
                far_re[re_row, re_lane] = 1
                far_re[im_row, im_lane] = 1
                far_im[im_row, re_lane] = 1
                far_im[re_row, im_lane] = -1
    return far_re, far_im


def cross_kernel(
    r_ref, blocks_ref, near_re_ref, near_im_ref, out_ref, wide_ref, own_ref, far_ref, near_ref, forms_ref, slots_ref
):
    slots_ref[...] = jnp.zeros_like(slots_ref)
    wide_ref[...] = r_ref[...].astype(F32)
    quarter = lax.broadcasted_iota(jnp.int32, (32, 128), 1) // 32
    for g4 in range(GROUPS // 4):
        for q4 in range(2):
            block = wide_ref[pl.ds(g4 * 128 * ROWS + q4, 128, stride=ROWS), :]
            own_ref[g4 * 128 : (g4 + 1) * 128, q4 * 128 : (q4 + 1) * 128] = block.astype(BF16)
            turned = block.T
            for g in range(4):
                rows = None
                for q in range(4):
                    piece = turned[q * 32 : (q + 1) * 32, :]
                    shift = ((q - g) * 32) % 128
                    if shift:
                        piece = pltpu.roll(piece, shift, 1)
                    rows = piece if rows is None else jnp.where(quarter == q, piece, rows)
                start = (g4 * 4 + g) * 32
                far_ref[start : start + 32, q4 * 128 : (q4 + 1) * 128] = rows
    for part, table in enumerate((near_re_ref, near_im_ref)):
        spread = jnp.dot(own_ref[...], table[...], preferred_element_type=F32)
        near_ref[part] = spread.astype(BF16)

    lane_j = lax.broadcasted_iota(jnp.int32, (32, 256), 1) // 16 % JJ
    keeps = [jnp.where(lane_j == j, 1.0, 0.0).astype(BF16) for j in range(JJ)]

    for g in range(GROUPS):
        far_rows = [(blocks_ref[g, k] + g * CG) & (GROUPS * CG - 1) for k in range(BLOCKS)]
        far = jnp.concatenate(
            [far_ref[pl.ds(pl.multiple_of(row, CB), CB), :] for row in far_rows], axis=0
        ).astype(BF16)
        sides = [near_ref[side, g * WIN : (g + 1) * WIN, :] for side in range(2)]
        near = jnp.concatenate([side * keep for keep in keeps for side in sides], axis=0)
        cross = jnp.dot(far, near, preferred_element_type=F32)
        for half in range(2):
            rows = cross[:, half * 128 : (half + 1) * 128]
            forms_ref[g, half * 256 : (half + 1) * 256, :] = rows
            forms_ref[g, (half + 2) * 256 : (half + 3) * 256, :] = pltpu.roll(rows, 64, 1)
        for k in range(BLOCKS):
            form = pl.multiple_of(blocks_ref[g, BLOCKS + k], CB)
            place = pl.multiple_of(blocks_ref[g, 2 * BLOCKS + k], CB)
            slots_ref[g, pl.ds(place, CB), :] = forms_ref[g, pl.ds(form, CB), :]
    first_half = lax.broadcasted_iota(jnp.int32, (256, 128), 1) < 64
    for g in range(GROUPS):
        low = slots_ref[g, :256, :]
        high = slots_ref[g, 256:, :]
        out_ref[g * 256 : (g + 1) * 256, :] = jnp.where(first_half, low, high).astype(BF16)


def cross(received, blocks):
    near_re, near_im = (jnp.asarray(t, BF16) for t in near_tables())
    vmem = pl.BlockSpec(memory_space=pltpu.VMEM)
    return pl.pallas_call(
        cross_kernel,
        out_shape=jax.ShapeDtypeStruct((GROUPS * 32 * CB, 128), BF16),
        in_specs=[vmem, pl.BlockSpec(memory_space=pltpu.SMEM), vmem, vmem],
        out_specs=vmem,
        scratch_shapes=[
            pltpu.VMEM((GROUPS * WIN * ROWS, 128), F32),
            pltpu.VMEM((512, 256), BF16),
            pltpu.VMEM((512, 256), F32),
            pltpu.VMEM((2, 512, 256), BF16),
            pltpu.VMEM((GROUPS, 4 * 256, 128), F32),
            pltpu.VMEM((GROUPS, SLOTS * 32 * CB, 128), F32),
        ],
        compiler_params=params(),
    )(received, blocks, near_re, near_im)


def lag_tables():
    shifts = np.arange(LAGS) - LAGS // 2
    angle = np.pi / F * (np.arange(PHI)[:, None] * shifts[None, :] % (2 * F))
    base = np.concatenate([np.cos(angle), np.sin(angle)], axis=1)
    high = base.astype(jnp.bfloat16)
    low = (base - high.astype(np.float64)).astype(jnp.bfloat16)
    turn = np.pi / F * (PHI * np.arange(JJ)[:, None] * shifts[None, :] % (2 * F))
    cos, sin = np.cos(turn), np.sin(turn)
    mix = np.stack([np.stack([cos, -sin], 1), np.stack([-sin, -cos], 1)], 1)
    mix = mix.reshape(JJ * 2 * 2, LAGS) / math.sqrt(F * WIN)
    return high, low, mix.astype(np.float32)


def lag_kernel(m_ref, high_ref, low_ref, mix_ref, out_ref, wide_ref):
    wide_ref[...] = m_ref[...].astype(F32)
    for far2 in range(CB // 2):
        rows = jnp.concatenate(
            [wide_ref[pl.ds(far2 * 2 + half, PHI, stride=CB), :].T for half in range(2)], axis=0
        ).astype(BF16)
        sums = jnp.dot(rows, high_ref[...], preferred_element_type=F32)
        sums = sums + jnp.dot(rows, low_ref[...], preferred_element_type=F32)
        for half in range(2):
            far = far2 * 2 + half
            for slot in range(SLOTS):
                total = None
                for q in range(JJ * 2):
                    start = half * 128 + slot * 64 + q * CB
                    rows_q = sums[start : start + CB]
                    term = rows_q[:, :LAGS] * mix_ref[2 * q : 2 * q + 1, :]
                    term = term + rows_q[:, LAGS:] * mix_ref[2 * q + 1 : 2 * q + 2, :]
                    total = term if total is None else total + term
                out_ref[slot, :, far * LAGS : (far + 1) * LAGS] = total


def lags(arrived):
    high, low, mix = lag_tables()
    return pl.pallas_call(
        lag_kernel,
        out_shape=jax.ShapeDtypeStruct((SLOTS, CB, CB * LAGS), F32),
        in_specs=[pl.BlockSpec(memory_space=pltpu.VMEM)] * 4,
        out_specs=pl.BlockSpec(memory_space=pltpu.VMEM),
        scratch_shapes=[
            pltpu.VMEM((PHI * CB, 128), F32),
        ],
        compiler_params=params(),
    )(arrived, jnp.asarray(high), jnp.asarray(low), jnp.asarray(mix))


def local(spectra, window_valid, pair_code, block_owner):
    both = ("chan", "tm")
    tiled = spectra.reshape(CG, 2, F // 128, 128).transpose(0, 2, 1, 3).reshape(CG * F // 64, 128)
    sent = whiten(tiled, window_valid, pair_code, block_owner).reshape(PHI, ROWS, 128)
    received = lax.all_to_all(sent, both, 0, 0, tiled=True)
    blocks = received[::WIN, 2].astype(jnp.int32) * CB
    crossed = cross(received.reshape(GROUPS * WIN * ROWS, 128), blocks)
    crossed = crossed.reshape(GROUPS * 32, CB, 128)
    arrived = lax.all_to_all(crossed, both, 0, 0, tiled=True).reshape(PHI * CB, 128)
    return lags(arrived)[None]


def solution(mesh):
    return jax.shard_map(
        local,
        mesh=mesh,
        in_specs=(P("tm", "chan", None, None), P("tm"), P("chan", None), P("chan", None)),
        out_specs=P("chan", "tm", None, None),
        check_vma=False,
    )
```

```python
import math

import jax
import jax.numpy as jnp
import numpy as np
from jax import lax
from jax.experimental import pallas as pl
from jax.experimental.pallas import tpu as pltpu
from jax.sharding import PartitionSpec as P

CB = 8
G = 4
CG = G * CB
LAGS = 256
SLOTS = 2
EPS = 1e-05
GROUPS = 16
WIN = 32
BLOCKS = 32
F = 2048
JJ = 4
PHI = F // JJ
MESSAGE = JJ * 2 * CG
ROWS = 4

BF16 = jnp.bfloat16
F32 = jnp.float32


def params():
    return pltpu.CompilerParams(vmem_limit_bytes=40 << 20)


def fields_kernel(code_ref, owner_ref, out_ref):
    lane = lax.broadcasted_iota(jnp.int32, (1, 128), 1)
    fill = jnp.full((1, 128 - BLOCKS), -1, jnp.int32)
    owner = jnp.concatenate([owner_ref[...], fill], axis=1)
    code = jnp.concatenate([code_ref[...], fill], axis=1)
    rank = jnp.zeros((1, 128), jnp.int32)
    for back in range(1, BLOCKS):
        same = pltpu.roll(owner, back, 1) == owner
        rank = rank + jnp.where(same & (lane >= back), 1, 0)
    near_blk = code // 36
    far = code - near_blk * 36
    form = ((near_blk >> 1) + 2 * ((near_blk & 1) ^ rank)) * BLOCKS + lane
    place = rank * 32 + owner
    fields = jnp.where(lane < BLOCKS, far, pltpu.roll(form, BLOCKS, 1))
    fields = jnp.where(lane < 2 * BLOCKS, fields, pltpu.roll(place, 2 * BLOCKS, 1))
    fields = jnp.where(lane < 3 * BLOCKS, fields, 0)
    out_ref[...] = fields.astype(F32)


def whiten_kernel(x_ref, valid_ref, fields_ref, out_ref, wide_ref, sent_ref):
    fields = jnp.broadcast_to(fields_ref[...], (PHI, 128))
    sent_ref[pl.ds(2, PHI, stride=ROWS), :] = fields
    sent_ref[pl.ds(3, PHI, stride=ROWS), :] = fields
    wide_ref[...] = x_ref[...].astype(F32)
    tiles = F // 128
    raw = [
        [wide_ref[pl.ds(tile * 2 + part, CG, stride=tiles * 2), :] for tile in range(tiles)]
        for part in range(2)
    ]
    squares = sum(block * block for side in raw for block in side)
    mean_power = jnp.sum(squares, axis=1, keepdims=True) * (1.0 / (2 * F))
    scale = lax.rsqrt(mean_power + EPS)
    valid = valid_ref[0].astype(F32)
    for pair in range(JJ // 2):
        for tile in range(PHI // 128):
            rows = jnp.concatenate(
                [
                    (raw[part][j * (PHI // 128) + tile] * scale).astype(BF16).astype(F32) * valid
                    for j in (2 * pair, 2 * pair + 1)
                    for part in range(2)
                ],
                axis=0,
            )
            sent_ref[pl.ds(tile * 128 * ROWS + pair, 128, stride=ROWS), :] = rows.T
    out_ref[...] = sent_ref[...].astype(BF16)


def whiten(spectra, valid, codes, owners):
    vmem = pl.BlockSpec(memory_space=pltpu.VMEM)
    fields = pl.pallas_call(
        fields_kernel,
        out_shape=jax.ShapeDtypeStruct((1, 128), F32),
        in_specs=[vmem] * 2,
        out_specs=vmem,
        compiler_params=params(),
        cost_estimate=pl.CostEstimate(flops=1 << 22, bytes_accessed=1 << 20, transcendentals=0),
    )(codes, owners)
    return pl.pallas_call(
        whiten_kernel,
        out_shape=jax.ShapeDtypeStruct((PHI * ROWS, 128), BF16),
        in_specs=[vmem, pl.BlockSpec(memory_space=pltpu.SMEM), vmem],
        out_specs=vmem,
        scratch_shapes=[
            pltpu.VMEM((CG * F // 64, 128), F32),
            pltpu.VMEM((PHI * ROWS, 128), F32),
        ],
        compiler_params=params(),
    )(spectra, valid, fields)


def near_tables():
    far_re = np.zeros((MESSAGE, 256), np.float32)
    far_im = np.zeros((MESSAGE, 256), np.float32)
    for r in range(G):
        for j in range(JJ):
            for i in range(CB):
                re_row = (j * 2) * CG + r * CB + i
                im_row = re_row + CG
                re_lane = r * 64 + (j * 2) * CB + i
                im_lane = re_lane + CB
                far_re[re_row, re_lane] = 1
                far_re[im_row, im_lane] = 1
                far_im[im_row, re_lane] = 1
                far_im[re_row, im_lane] = -1
    return far_re, far_im


def cross_kernel(
    r_ref, blocks_ref, near_re_ref, near_im_ref, out_ref, wide_ref, own_ref, far_ref, near_ref, forms_ref, slots_ref
):
    wide_ref[...] = r_ref[...].astype(F32)
    quarter = lax.broadcasted_iota(jnp.int32, (32, 128), 1) // 32
    for g4 in range(GROUPS // 4):
        for q4 in range(2):
            block = wide_ref[pl.ds(g4 * 128 * ROWS + q4, 128, stride=ROWS), :]
            own_ref[g4 * 128 : (g4 + 1) * 128, q4 * 128 : (q4 + 1) * 128] = block.astype(BF16)
            turned = block.T
            for g in range(4):
                rows = None
                for q in range(4):
                    piece = turned[q * 32 : (q + 1) * 32, :]
                    shift = ((q - g) * 32) % 128
                    if shift:
                        piece = pltpu.roll(piece, shift, 1)
                    rows = piece if rows is None else jnp.where(quarter == q, piece, rows)
                start = (g4 * 4 + g) * 32
                far_ref[start : start + 32, q4 * 128 : (q4 + 1) * 128] = rows
    for part, table in enumerate((near_re_ref, near_im_ref)):
        spread = jnp.dot(own_ref[...], table[...], preferred_element_type=F32)
        near_ref[part] = spread.astype(BF16)

    lane_j = lax.broadcasted_iota(jnp.int32, (32, 256), 1) // 16 % JJ
    keeps = [jnp.where(lane_j == j, 1.0, 0.0).astype(BF16) for j in range(JJ)]

    for g in range(GROUPS):
        slots_ref[g] = jnp.zeros((SLOTS * 32 * CB, 128), F32)
        far_rows = [(blocks_ref[g, k] + g * CG) & (GROUPS * CG - 1) for k in range(BLOCKS)]
        far = jnp.concatenate(
            [far_ref[pl.ds(pl.multiple_of(row, CB), CB), :] for row in far_rows], axis=0
        ).astype(BF16)
        sides = [near_ref[side, g * WIN : (g + 1) * WIN, :] for side in range(2)]
        near = jnp.concatenate([side * keep for keep in keeps for side in sides], axis=0)
        cross = jnp.dot(far, near, preferred_element_type=F32)
        for half in range(2):
            rows = cross[:, half * 128 : (half + 1) * 128]
            forms_ref[g, half * 256 : (half + 1) * 256, :] = rows
            forms_ref[g, (half + 2) * 256 : (half + 3) * 256, :] = pltpu.roll(rows, 64, 1)
        for k in range(BLOCKS):
            form = pl.multiple_of(blocks_ref[g, BLOCKS + k], CB)
            place = pl.multiple_of(blocks_ref[g, 2 * BLOCKS + k], CB)
            slots_ref[g, pl.ds(place, CB), :] = forms_ref[g, pl.ds(form, CB), :]
    first_half = lax.broadcasted_iota(jnp.int32, (256, 128), 1) < 64
    for g in range(GROUPS):
        low = slots_ref[g, :256, :]
        high = slots_ref[g, 256:, :]
        out_ref[g * 256 : (g + 1) * 256, :] = jnp.where(first_half, low, high).astype(BF16)


def cross(received, blocks):
    near_re, near_im = (jnp.asarray(t, BF16) for t in near_tables())
    vmem = pl.BlockSpec(memory_space=pltpu.VMEM)
    return pl.pallas_call(
        cross_kernel,
        out_shape=jax.ShapeDtypeStruct((GROUPS * 32 * CB, 128), BF16),
        in_specs=[vmem, pl.BlockSpec(memory_space=pltpu.SMEM), vmem, vmem],
        out_specs=vmem,
        scratch_shapes=[
            pltpu.VMEM((GROUPS * WIN * ROWS, 128), F32),
            pltpu.VMEM((512, 256), BF16),
            pltpu.VMEM((512, 256), F32),
            pltpu.VMEM((2, 512, 256), BF16),
            pltpu.VMEM((GROUPS, 4 * 256, 128), F32),
            pltpu.VMEM((GROUPS, SLOTS * 32 * CB, 128), F32),
        ],
        compiler_params=params(),
    )(received, blocks, near_re, near_im)


def lag_tables():
    shifts = np.arange(LAGS) - LAGS // 2
    angle = np.pi / F * (np.arange(PHI)[:, None] * shifts[None, :] % (2 * F))
    base = np.concatenate([np.cos(angle), np.sin(angle)], axis=1)
    high = base.astype(jnp.bfloat16)
    low = (base - high.astype(np.float64)).astype(jnp.bfloat16)
    turn = np.pi / F * (PHI * np.arange(JJ)[:, None] * shifts[None, :] % (2 * F))
    cos, sin = np.cos(turn), np.sin(turn)
    mix = np.stack([np.stack([cos, -sin], 1), np.stack([-sin, -cos], 1)], 1)
    mix = mix.reshape(JJ * 2 * 2, LAGS) / math.sqrt(F * WIN)
    return high, low, mix.astype(np.float32)


def lag_kernel(m_ref, high_ref, low_ref, mix_ref, out_ref, wide_ref):
    wide_ref[...] = m_ref[...].astype(F32)
    for far2 in range(CB // 2):
        rows = jnp.concatenate(
            [wide_ref[pl.ds(far2 * 2 + half, PHI, stride=CB), :].T for half in range(2)], axis=0
        ).astype(BF16)
        sums = jnp.dot(rows, high_ref[...], preferred_element_type=F32)
        sums = sums + jnp.dot(rows, low_ref[...], preferred_element_type=F32)
        for half in range(2):
            far = far2 * 2 + half
            for slot in range(SLOTS):
                total = None
                for q in range(JJ * 2):
                    start = half * 128 + slot * 64 + q * CB
                    rows_q = sums[start : start + CB]
                    term = rows_q[:, :LAGS] * mix_ref[2 * q : 2 * q + 1, :]
                    term = term + rows_q[:, LAGS:] * mix_ref[2 * q + 1 : 2 * q + 2, :]
                    total = term if total is None else total + term
                out_ref[slot, :, far * LAGS : (far + 1) * LAGS] = total


def lags(arrived):
    high, low, mix = lag_tables()
    return pl.pallas_call(
        lag_kernel,
        out_shape=jax.ShapeDtypeStruct((SLOTS, CB, CB * LAGS), F32),
        in_specs=[pl.BlockSpec(memory_space=pltpu.VMEM)] * 4,
        out_specs=pl.BlockSpec(memory_space=pltpu.VMEM),
        scratch_shapes=[
            pltpu.VMEM((PHI * CB, 128), F32),
        ],
        compiler_params=params(),
    )(arrived, jnp.asarray(high), jnp.asarray(low), jnp.asarray(mix))


def local(spectra, window_valid, pair_code, block_owner):
    both = ("chan", "tm")
    tiled = spectra.reshape(CG, 2, F // 128, 128).transpose(0, 2, 1, 3).reshape(CG * F // 64, 128)
    sent = whiten(tiled, window_valid, pair_code, block_owner).reshape(PHI, ROWS, 128)
    received = lax.all_to_all(sent, both, 0, 0, tiled=True)
    blocks = received[::WIN, 2].astype(jnp.int32) * CB
    crossed = cross(received.reshape(GROUPS * WIN * ROWS, 128), blocks)
    crossed = crossed.reshape(GROUPS * 32, CB, 128)
    arrived = lax.all_to_all(crossed, both, 0, 0, tiled=True).reshape(PHI * CB, 128)
    return lags(arrived)[None]


def solution(mesh):
    return jax.shard_map(
        local,
        mesh=mesh,
        in_specs=(P("tm", "chan", None, None), P("tm"), P("chan", None), P("chan", None)),
        out_specs=P("chan", "tm", None, None),
        check_vma=False,
    )
```
